32 devices in a mesh: wide: 8 (over z, y), narrow: 4 (over x, core).
Axes of the slice: x: 2, y: 2, z: 4, core: 2. Of those that a mesh axis runs over, the one named last changes fastest.
Arguments:
- tokens: bfloat16 [32768, 768], P(('wide', 'narrow')), may hold values from -6 to 6
- gain_one: float32 [768], replicated, may hold values from 0.5 to 1.5
- w_query: bfloat16 [768, 768], replicated, may hold values from -0.21875 to 0.21875
- w_key: bfloat16 [768, 768], replicated, may hold values from -0.21875 to 0.21875
- w_value: bfloat16 [768, 768], replicated, may hold values from -0.21875 to 0.21875
- w_out: bfloat16 [768, 768], replicated, may hold values from -1.75 to 1.75
- table: float32 [32, 12], replicated, may hold values from -4 to 4
- gain_two: float32 [768], replicated, may hold values from 0.5 to 1.5
- w_router: bfloat16 [768, 32], replicated, may hold values from -0.109375 to 0.109375
- w_up: bfloat16 [32, 768, 3072], P(('wide', 'narrow')), may hold values from -0.21875 to 0.21875
- w_down: bfloat16 [32, 3072, 768], P(('wide', 'narrow')), may hold values from -8 to 8
- routes: int32 [32768, 1], P(('wide', 'narrow')), may hold values from 0 to 31; in each aligned block of 1024 rows (0 to 1023, 1024 to 2047, ...) at most 80 rows name the same one
- cotangent: bfloat16 [32768, 768], P(('wide', 'narrow')), may hold values from -6 to 6
Outputs:
- output: bfloat16 [32768, 768], P(('wide', 'narrow'))
- tokens_grad: bfloat16 [32768, 768], P(('wide', 'narrow'))
- gain_one_grad: float32 [768], replicated
- query_grad: float32 [768, 768], replicated
- key_grad: float32 [768, 768], replicated
- value_grad: float32 [768, 768], replicated
- out_grad: float32 [768, 768], replicated
- table_grad: float32 [32, 12], replicated
- gain_two_grad: float32 [768], replicated
- router_grad: float32 [768, 32], replicated
- up_grad: float32 [32, 768, 3072], P(('wide', 'narrow'))
- down_grad: float32 [32, 3072, 768], P(('wide', 'narrow'))
The draws below stay inside these ranges and needn't reach their ends.
Inputs may be any that keep to these rules, and one draw needn't show every extreme that they name: `routes`: each token names one expert. Among the 1024 tokens of one device no expert is named more than 2 * 40 times, and in every draw some device names some expert exactly 2 * 40 times.
All inputs are finite; a program needn't handle non-finite values.
Results may differ from the reference program's by a relative error of at most 0.018.
Values may be sent and summed in bfloat16 or wider, within the bound.
A program may use at most 256 MiB of HBM per device.

```python
import math
import jax
import jax.numpy as jnp
import numpy as np
from jax import lax

D = 768
HEADS = 12
HEAD_DIM = 64
FF = 3072
BUCKETS = 32
SEQ_LEN = 512
TOK_DEV = 1024
TOKENS = 32768
EXPERTS = 32
CAP = 40
N_WIDE = 8
N_NARROW = 4


def shard_levels(rng, shape, shards, smallest, largest):
    factor_of, own = 1.0, jax.random.fold_in(rng, 6)
    for position, blocks in shards:
        draws = jnp.exp(jax.random.uniform(jax.random.fold_in(own, position), (blocks,), jnp.float32, smallest / len(shards), largest / len(shards)))
        factor_of = factor_of * jnp.repeat(draws, shape[position] // blocks).reshape([-1 if axis == position else 1 for axis in range(len(shape))])
    return factor_of


def routed_block(stream_key, own, number, rows, amount, top, most, lean):
    sequence = jax.random.permutation(stream_key, amount)
    packed, ordinary = portions_of(amount, rows * top, most, lean, True), portions_of(amount, rows * top, most, lean, False)
    places = jnp.arange(amount)

    def named(tallies, turn):
        used = int((tallies > 0).sum())
        fixed = max(1, used // 4)
        passed = fixed + (places - fixed + turn * (used - fixed)) % max(1, amount - fixed)
        return jnp.zeros((amount,), jnp.int32).at[sequence[jnp.where(places < fixed, places, passed)]].set(jnp.asarray(tallies, jnp.int32))

    tallies = jnp.where(number % 4 == 0, named(packed, number // 4), named(ordinary, number - number // 4 - 1))
    mixed = jax.random.permutation(jax.random.fold_in(own, 3), amount)
    donor, sink = mixed[0:amount // 2 * 2:2], mixed[1:amount // 2 * 2:2]
    margin = jnp.minimum(tallies[donor] - 1, most - tallies[sink]) // 2
    margin = jnp.where((donor == sequence[0]) | (sink == sequence[0]) | (tallies[sink] == 0), 0, jnp.maximum(margin, 0))
    passed = jax.random.randint(jax.random.fold_in(own, 4), (amount // 2,), 0, 1 << 20) % (margin + 1)
    tallies = tallies.at[donor].add(-passed).at[sink].add(passed)
    labels = jnp.searchsorted(jnp.cumsum(tallies), jnp.arange(rows * top), side="right").astype(jnp.int32)
    table = labels.reshape(top, rows).T
    table = table[jax.random.permutation(jax.random.fold_in(own, 1), rows)]
    turn = jax.random.randint(jax.random.fold_in(own, 2), (rows, 1), 0, top)
    return jnp.take_along_axis(table, (jnp.arange(top)[None, :] + turn) % top, axis=1)


def portions_of(number_of, total, most, skew, full):
    loads = [(1 << 20) // math.isqrt(rank ** skew) + 1 for rank in range(1, number_of + 1)]
    largest = most if full else min(most, max(-(-total // number_of), total * loads[0] // sum(loads)))
    least = 1 if total - largest >= number_of - 1 else 0
    holding, rest = [largest] + [least] * (number_of - 1), total - largest - least * (number_of - 1)
    while rest > 0:
        candidates = [i for i in range(1, number_of) if holding[i] < largest] or [i for i in range(1, number_of) if holding[i] < most]
        mass, left = sum([loads[i] for i in candidates]), rest
        for i in candidates:
            extra = min(most - holding[i], max(1, left * loads[i] // mass), rest)
            holding[i] = holding[i] + extra
            rest = rest - extra
    return np.array(holding)


def scatter_about(rng, extent, deviation, bound, shards=(), held_as=jnp.bfloat16):
    values = deviation * jax.random.normal(rng, extent, jnp.float32)
    if shards:
        values = values * shard_levels(rng, extent, shards, -0.22, 0.18)
    return jnp.clip(values, -bound, bound).astype(held_as)


def setup_inputs(seed: int = 0) -> dict:
    arg_keys = jax.random.split(jax.random.key(seed), 14)
    tokens = scatter_about(arg_keys[0], (TOKENS, D), 1.0, 6.0, ((0, 32),))
    gain_one = jnp.clip(1.0 + 0.1 * jax.random.normal(arg_keys[1], (D,), jnp.float32), 0.5, 1.5)
    w_query = scatter_about(arg_keys[2], (D, D), D ** -0.5, 0.21875)
    w_key = scatter_about(arg_keys[3], (D, D), D ** -0.5, 0.21875)
    w_value = scatter_about(arg_keys[4], (D, D), D ** -0.5, 0.21875)
    w_out = scatter_about(arg_keys[5], (D, D), (D // 64) ** -0.5, 1.75)
    table = scatter_about(arg_keys[6], (BUCKETS, HEADS), 1.0, 4.0, (), jnp.float32)
    gain_two = jnp.clip(1.0 + 0.1 * jax.random.normal(arg_keys[7], (D,), jnp.float32), 0.5, 1.5)
    w_router = scatter_about(arg_keys[8], (D, EXPERTS), (4 * D) ** -0.5, 0.109375)
    w_up = scatter_about(arg_keys[9], (EXPERTS, D, FF), D ** -0.5, 0.21875, ((0, 32),))
    w_down = scatter_about(arg_keys[10], (EXPERTS, FF, D), (0.045 * EXPERTS), 8.0, ((0, 32),))
    routes_keys = jax.random.split(jax.random.fold_in(arg_keys[11], 1), TOKENS // TOK_DEV)
    routes_turns = jax.random.permutation(jax.random.fold_in(arg_keys[11], 3), TOKENS // TOK_DEV)
    routes = jax.vmap(lambda own, number: routed_block(jax.random.fold_in(arg_keys[11], 2), own, number, TOK_DEV, EXPERTS, 1, 2 * CAP, 1))(routes_keys, routes_turns).reshape((TOKENS, 1))
    cotangent = scatter_about(arg_keys[12], (TOKENS, D), 1.0, 6.0, ((0, 32),))
    return dict(tokens=tokens, gain_one=gain_one, w_query=w_query, w_key=w_key, w_value=w_value, w_out=w_out, table=table, gain_two=gain_two, w_router=w_router, w_up=w_up, w_down=w_down, routes=routes, cotangent=cotangent)


@jax.custom_vjp
def low(v):
    return lax.optimization_barrier(v.astype(jnp.bfloat16)).astype(jnp.float32)

@jax.custom_vjp
def low_back(v):
    return v

def low_keep(v):
    return (low(v), None)

def low_pass(kept, grad):
    return (grad,)

def back_keep(v):
    return (v, None)

def back_low(kept, grad):
    return (low(grad),)
low.defvjp(low_keep, low_pass)
low_back.defvjp(back_keep, back_low)
EPSILON = 1e-06
LIMITS = (12, 16, 23, 32, 46, 64, 91)
HIGHEST = lax.Precision.HIGHEST

def bucket_index(length):
    places = jnp.arange(length, dtype=jnp.int32)
    offset = places[None, :] - places[:, None]
    distance = jnp.abs(offset)
    further = 8 + sum(((distance >= limit).astype(jnp.int32) for limit in LIMITS))
    nearby = jnp.where(distance < 8, distance, further)
    return (nearby + 16 * (offset > 0).astype(jnp.int32)).astype(jnp.int32)

def norm_gain(values, gain):
    factor = lax.rsqrt(lax.optimization_barrier(jnp.mean(values * values, axis=-1, keepdims=True)) + EPSILON)
    return values * factor * gain

def product_exact(left, right):
    return jnp.matmul(left, right, precision=HIGHEST)

def attention_block(block_in, params):
    gain_one, w_query, w_key, w_value, w_out, bias = params
    group = block_in.shape[0]
    shaped = (group, SEQ_LEN, HEADS, HEAD_DIM)
    normed = low(norm_gain(block_in, gain_one))
    query = low(low_back(product_exact(normed, w_query))).reshape(shaped)
    key = low(low_back(product_exact(normed, w_key))).reshape(shaped)
    value = low(low_back(product_exact(normed, w_value))).reshape(shaped)
    scores = jnp.einsum('glhd,gmhd->ghlm', query, key, precision=HIGHEST) * HEAD_DIM ** (-0.5) + bias[None]
    scores = low_back(scores)
    weights = low(jax.nn.softmax(scores, axis=-1))
    mixed = jnp.einsum('ghlm,gmhd->glhd', weights, value, precision=HIGHEST).reshape(group, SEQ_LEN, HEADS * HEAD_DIM)
    mixed = low(low_back(mixed))
    return block_in + low_back(product_exact(mixed, w_out))

def expert_apply(item):
    rows, w_first, w_second = item
    raised = low_back(product_exact(rows, w_first))
    active = low(jax.nn.gelu(raised, approximate=True))
    return low(low_back(product_exact(active, w_second)))

def forward(inputs, gain_one, w_query, w_key, w_value, w_out, table, gain_two, w_router, w_up, w_down, chosen):
    bias = jnp.transpose(table[bucket_index(SEQ_LEN)], (2, 0, 1))
    sequences = TOKENS // SEQ_LEN
    group = math.gcd(sequences, max(1, 4096 // SEQ_LEN))
    blocks = inputs.reshape(sequences // group, group, SEQ_LEN, D)
    params = (gain_one, w_query, w_key, w_value, w_out, bias)
    hidden = lax.map(jax.checkpoint(lambda block_in: attention_block(block_in, params)), blocks).reshape(TOKENS, D)
    normed = low(norm_gain(hidden, gain_two))
    logits = low_back(product_exact(normed, w_router))
    probs = jax.nn.softmax(logits, axis=-1)
    picks = chosen[:, None] == jnp.arange(EXPERTS, dtype=jnp.int32)[None, :]
    gate = lax.optimization_barrier(jnp.sum(jnp.where(picks, probs, jnp.zeros_like(probs)), axis=-1))
    sources = N_WIDE * N_NARROW
    counts = picks.astype(jnp.int32).reshape(sources, TOK_DEV, EXPERTS)
    earlier = jnp.cumsum(counts, axis=1) - counts
    slot = lax.optimization_barrier(jnp.sum(earlier * counts, axis=-1)).reshape(TOKENS)
    anchor = jnp.arange(TOKENS, dtype=jnp.int32) // TOK_DEV
    rows_all = EXPERTS * sources * CAP
    target = jnp.where(slot < CAP, (chosen * sources + anchor) * CAP + slot, rows_all).astype(jnp.int32)
    buffer = jnp.zeros((rows_all + 1, D), inputs.dtype).at[target].add(normed)[:rows_all]
    buffer = low_back(buffer).reshape(EXPERTS, sources * CAP, D)
    produced = lax.map(jax.checkpoint(expert_apply), (buffer, w_up, w_down))
    padded = jnp.concatenate([produced.reshape(rows_all, D), jnp.zeros((1, D), produced.dtype)], axis=0)
    returned = padded[target]
    return hidden + gate[:, None] * returned

def reference(tokens, gain_one, w_query, w_key, w_value, w_out, table, gain_two, w_router, w_up, w_down, routes, cotangent):
    chosen = routes[:, 0].astype(jnp.int32)
    floats = [array.astype(jnp.float32) for array in (tokens, gain_one, w_query, w_key, w_value, w_out, table, gain_two, w_router, w_up, w_down)]
    result, pullback = jax.vjp(lambda *values: forward(*values, chosen), *floats)
    grads = pullback(cotangent.astype(jnp.float32))
    return (result.astype(jnp.bfloat16), grads[0].astype(jnp.bfloat16), grads[1], grads[2], grads[3], grads[4], grads[5], grads[6], grads[7], grads[8], grads[9], grads[10])
```

```python
import functools

import jax
import jax.numpy as jnp
import numpy as np
from jax import lax
from jax.experimental import pallas as pl
from jax.experimental.pallas import tpu as pltpu
from jax.sharding import PartitionSpec as P

HEADS = 12
HEAD_DIM = 64
BUCKETS = 32
SEQ_LEN = 512
EPSILON = 1e-06
LIMITS = (12, 16, 23, 32, 46, 64, 91)
HIGHEST = lax.Precision.HIGHEST
MESH = pl.DeviceIdType.MESH
BOTH = ("wide", "narrow")
GROUP = 4
COLUMNS = GROUP * HEAD_DIM
TILE = 128
SPAN = 512
HALF = 256
VMEM_LIMIT = 56 * 2**20

bf16 = jnp.bfloat16
f32 = jnp.float32


def product(left, right, **options):
    return jnp.dot(left, right, preferred_element_type=f32, **options)


def product_left(left, right, **options):
    return lax.dot_general(left, right, (((0,), (0,)), ((), ())), preferred_element_type=f32, **options)


def product_right(left, right, **options):
    return lax.dot_general(left, right, (((1,), (1,)), ((), ())), preferred_element_type=f32, **options)


def gelu_curve(values):
    return jax.nn.gelu(values, approximate=True)


def lane_buckets():
    offset = SPAN // 2 - np.arange(SPAN)
    distance = np.abs(offset)
    further = 8 + sum((distance >= limit).astype(np.int32) for limit in LIMITS)
    bucket = np.where(distance < 8, distance, further) + 16 * (offset > 0)
    return (bucket[:, None] == np.arange(BUCKETS)[None, :]).astype(np.float32)


def whole(shape):
    return pl.BlockSpec(shape, lambda *_: (0,) * len(shape))


def slots_kernel(capacity, column_ref, row_ref, rows_ref, target_column_ref, target_row_ref, sent_ref):
    count = column_ref.shape[0]
    experts = sent_ref.shape[0] // capacity
    token_down = lax.broadcasted_iota(jnp.int32, (count, count), 0)
    token_across = lax.broadcasted_iota(jnp.int32, (count, count), 1)
    column = column_ref[...]
    picks = column == lax.broadcasted_iota(jnp.int32, (count, experts), 1)
    earlier = (token_down > token_across).astype(bf16)
    before = product(earlier, picks.astype(bf16))
    slot = jnp.sum(jnp.where(picks, before, 0.0), axis=1, keepdims=True).astype(jnp.int32)
    target_column_ref[...] = jnp.where(slot < capacity, column * capacity + slot, -1)
    row = row_ref[...]
    picks = row == lax.broadcasted_iota(jnp.int32, (experts, count), 0)
    earlier = (token_down < token_across).astype(bf16)
    before = product(picks.astype(bf16), earlier)
    slot = jnp.sum(jnp.where(picks, before, 0.0), axis=0, keepdims=True).astype(jnp.int32)
    target = jnp.where(slot < capacity, row * capacity + slot, -1)
    target_row_ref[...] = target
    place_rows(target, rows_ref, sent_ref)


def place_rows(target, rows_ref, sent_ref):
    total, count = sent_ref.shape[0], rows_ref.shape[0]
    piece = total // 4

    def body(index, carry):
        start = pl.multiple_of(index * piece, 16)
        slots = start + lax.broadcasted_iota(jnp.int32, (piece, count), 0)
        placing = (slots == target).astype(bf16)
        sent_ref[pl.ds(start, piece), :] = product(placing, rows_ref[...]).astype(bf16)
        return carry

    lax.fori_loop(0, total // piece, body, 0)


def forward_kernel(
    capacity,
    tokens_ref,
    gain_one_ref,
    w_query_ref,
    w_key_ref,
    w_value_ref,
    w_out_ref,
    table_ref,
    buckets_ref,
    far_ref,
    gain_two_ref,
    w_router_ref,
    column_ref,
    target_ref,
    hidden_ref,
    normed_ref,
    normed_t_ref,
    query_ref,
    key_t_ref,
    value_ref,
    weights_ref,
    mixed_t_ref,
    normed_two_ref,
    probs_ref,
    gate_ref,
    sent_ref,
    curves,
    key_rows,
    query_t,
    value_t,
):
    group = pl.program_id(0)
    count, width = tokens_ref.shape
    sequences = count // SEQ_LEN

    @pl.when(group == 0)
    def _():
        inputs = tokens_ref[...].astype(f32)
        factor = lax.rsqrt(jnp.mean(inputs * inputs, axis=1, keepdims=True) + EPSILON)
        normed = (inputs * factor * gain_one_ref[...]).astype(bf16)
        normed_ref[...] = normed
        normed_t_ref[...] = normed.T
        hidden_ref[...] = inputs
        curve = lax.dot_general(
            table_ref[...], buckets_ref[...], (((0,), (1,)), ((), ())), preferred_element_type=f32, precision=HIGHEST
        )
        for head in range(HEADS):
            wide = jnp.broadcast_to(curve[head : head + 1, :], (TILE, SPAN))
            curves[head] = pltpu.roll(wide, 0, 1, stride=1, stride_axis=0)

    normed = normed_ref[...]
    query = product(normed, w_query_ref[...]).astype(bf16)
    query_ref[...] = query
    query_t[...] = (query * jnp.asarray(HEAD_DIM**-0.5, bf16)).T
    key = product(normed, w_key_ref[...]).astype(bf16)
    key_rows[...] = key
    key_t_ref[...] = key.T
    value = product(normed, w_value_ref[...]).astype(bf16)
    value_ref[...] = value
    value_t[...] = value.T

    lane = lax.broadcasted_iota(jnp.int32, (SEQ_LEN, TILE), 1)
    for head in range(GROUP):
        pair = head // 2 * TILE
        mine = (lane // HEAD_DIM) == head % 2
        index = group * GROUP + head
        far_left = far_ref[15, index]
        far_right = far_ref[31, index]
        for sequence in range(sequences):
            rows = pl.ds(sequence * SEQ_LEN, SEQ_LEN)
            keys = jnp.where(mine, key_rows[rows, pair : pair + TILE], jnp.zeros((), bf16))
            for half in range(SEQ_LEN // HALF):
                columns = pl.ds(sequence * SEQ_LEN + half * HALF, HALF)
                raw = product(keys, query_t[pair : pair + TILE, columns])
                parts = []
                for down in range(SEQ_LEN // TILE):
                    line = []
                    for across in range(HALF // TILE):
                        step = down - (half * (HALF // TILE) + across)
                        block = raw[down * TILE : (down + 1) * TILE, across * TILE : (across + 1) * TILE]
                        if abs(step) <= 1:
                            begin = SPAN // 2 - step * TILE
                            bias = curves[index, :, begin : begin + TILE]
                        else:
                            bias = far_right if step > 0 else far_left
                        line.append(block + bias)
                    parts.append(jnp.concatenate(line, axis=1))
                scores = jnp.concatenate(parts, axis=0)
                maximum = jnp.max(scores, axis=0, keepdims=True)
                exponent = jnp.exp(scores - maximum)
                total = jnp.sum(exponent, axis=0, keepdims=True)
                weights = (exponent * (1.0 / total)).astype(bf16)
                weights_ref[head, sequence, :, half * HALF : (half + 1) * HALF] = weights
                mixed_t_ref[head * HEAD_DIM : (head + 1) * HEAD_DIM, columns] = product(
                    value_t[head * HEAD_DIM : (head + 1) * HEAD_DIM, rows], weights
                ).astype(bf16)
    hidden_ref[...] += product(mixed_t_ref[...].T, w_out_ref[...])

    @pl.when(group == pl.num_programs(0) - 1)
    def _():
        hidden = hidden_ref[...]
        factor = lax.rsqrt(jnp.mean(hidden * hidden, axis=1, keepdims=True) + EPSILON)
        normed_two = (hidden * factor * gain_two_ref[...]).astype(bf16)
        normed_two_ref[...] = normed_two
        logits = product(normed_two, w_router_ref[...])
        exponent = jnp.exp(logits - jnp.max(logits, axis=1, keepdims=True))
        probs = exponent / jnp.sum(exponent, axis=1, keepdims=True)
        probs_ref[...] = probs
        picks = column_ref[...] == lax.broadcasted_iota(jnp.int32, probs.shape, 1)
        gate_ref[...] = jnp.sum(jnp.where(picks, probs, 0.0), axis=1, keepdims=True)
        place_rows(target_ref[...], normed_two_ref, sent_ref)


def backward_kernel(
    mixed_bar_ref,
    mixed_bar_t_ref,
    query_ref,
    key_t_ref,
    value_ref,
    weights_ref,
    normed_t_ref,
    w_query_ref,
    w_key_ref,
    w_value_ref,
    buckets_ref,
    query_grad_ref,
    key_grad_ref,
    value_grad_ref,
    normed_bar_ref,
    table_grad_ref,
    scores_s,
    query_bar_t,
    key_bar,
    value_bar,
    near,
    far,
    diagonals,
):
    group = pl.program_id(0)
    count, width = normed_bar_ref.shape
    sequences = count // SEQ_LEN
    scale = HEAD_DIM**-0.5

    @pl.when(group == 0)
    def _():
        diagonals[...] = jnp.zeros_like(diagonals)

    lane = lax.broadcasted_iota(jnp.int32, (SEQ_LEN, TILE), 1)
    for head in range(GROUP):
        pair = head // 2 * TILE
        mine = (lane // HEAD_DIM) == head % 2
        feature = pl.ds(head * HEAD_DIM, HEAD_DIM)
        near[...] = jnp.zeros_like(near)
        far[...] = jnp.zeros_like(far)
        for sequence in range(sequences):
            rows = pl.ds(sequence * SEQ_LEN, SEQ_LEN)
            values = jnp.where(mine, value_ref[rows, pair : pair + TILE], jnp.zeros((), bf16))
            for half in range(SEQ_LEN // HALF):
                columns = pl.ds(sequence * SEQ_LEN + half * HALF, HALF)
                probs_bar = product(values, mixed_bar_t_ref[pair : pair + TILE, columns])
                probs = weights_ref[head, sequence, :, half * HALF : (half + 1) * HALF].astype(f32)
                shared = probs * probs_bar
                total = jnp.sum(shared, axis=0, keepdims=True)
                scores_bar = shared - probs * total
                scores_s[:, half * HALF : (half + 1) * HALF] = scores_bar.astype(bf16)
                for down in range(SEQ_LEN // TILE):
                    for across in range(HALF // TILE):
                        step = down - (half * (HALF // TILE) + across)
                        block = scores_bar[down * TILE : (down + 1) * TILE, across * TILE : (across + 1) * TILE]
                        if abs(step) <= 1:
                            begin = SPAN // 2 - step * TILE
                            near[:, begin : begin + TILE] += block
                        else:
                            side = 1 if step > 0 else 0
                            far[side] += jnp.sum(block.reshape(TILE // 8, 8, TILE), axis=0)
            weights = weights_ref[head, sequence]
            scores_low = scores_s[...]
            value_part = product(weights, mixed_bar_ref[rows, pair : pair + TILE]).astype(bf16)
            key_part = (product(scores_low, query_ref[rows, pair : pair + TILE]) * scale).astype(bf16)
            if head % 2 == 0:
                value_bar[rows, pair : pair + TILE] = value_part
                key_bar[rows, pair : pair + TILE] = key_part
            else:
                value_bar[rows, pair : pair + TILE] = jnp.where(mine, value_part, value_bar[rows, pair : pair + TILE])
                key_bar[rows, pair : pair + TILE] = jnp.where(mine, key_part, key_bar[rows, pair : pair + TILE])
            query_bar_t[feature, rows] = (product(key_t_ref[feature, rows], scores_low) * scale).astype(bf16)
        folded = near[0:8, :]
        for step in range(1, TILE // 8):
            folded = folded + pltpu.roll(near[8 * step : 8 * step + 8, :], SPAN - 8 * step, 1)
        place = lax.broadcasted_iota(jnp.int32, (8, SPAN), 0)
        for bit in (4, 2, 1):
            folded = jnp.where((place & bit) > 0, pltpu.roll(folded, SPAN - bit, 1), folded)
        gathered = jnp.sum(folded, axis=0, keepdims=True)
        place = lax.broadcasted_iota(jnp.int32, (1, SPAN), 1)
        left = jnp.sum(far[0])
        right = jnp.sum(far[1])
        gathered = gathered + jnp.where(place == SPAN - 1, left, 0.0) + jnp.where(place == 0, right, 0.0)
        diagonals[pl.ds(group * GROUP + head, 1), :] = gathered
    query_bar = query_bar_t[...].T
    normed_t = normed_t_ref[...]
    query_grad_ref[...] = product(normed_t, query_bar).astype(query_grad_ref.dtype)
    key_grad_ref[...] = product(normed_t, key_bar[...]).astype(key_grad_ref.dtype)
    value_grad_ref[...] = product(normed_t, value_bar[...]).astype(value_grad_ref.dtype)
    normed_bar = (
        product_right(query_bar, w_query_ref[...])
        + product_right(key_bar[...], w_key_ref[...])
        + product_right(value_bar[...], w_value_ref[...])
    )

    @pl.when(group == 0)
    def _():
        normed_bar_ref[...] = normed_bar

    @pl.when(group > 0)
    def _():
        normed_bar_ref[...] += normed_bar

    @pl.when(group == pl.num_programs(0) - 1)
    def _():
        table_grad_ref[...] = product(diagonals[...], buckets_ref[...], precision=HIGHEST)


def partner_of(axis, bit):
    w, k = lax.axis_index("wide"), lax.axis_index("narrow")
    place = w if axis == "wide" else k
    own = (place // bit) % 2
    other = place + bit - 2 * bit * own
    return own, ((other, k) if axis == "wide" else (w, other))


def bits_of(n_wide, n_narrow):
    narrow = [("narrow", 1 << b) for b in range(n_narrow.bit_length() - 1)]
    wide = [("wide", 1 << b) for b in range(n_wide.bit_length() - 1)]
    return narrow + wide


HALVINGS = 5


class Reduction:
    def __init__(self, buffer, gathered, received, send, receive, order, lanes_first):
        self.buffer, self.gathered, self.received = buffer, gathered, received
        self.send, self.receive = send, receive
        self.order, self.halvings = order, min(HALVINGS, len(order))
        rows, lanes = buffer.shape
        self.regions = [((0, rows), (0, lanes))]
        self.others = []
        self.lanes_first = lanes_first
        for step in range(self.halvings):
            own, _ = partner_of(*order[step])
            (row, rows), (lane, lanes) = self.regions[-1]
            if step == 0 and lanes_first:
                lanes = lanes // 2
                self.others.append(((row, rows), (lane + (1 - own) * lanes, lanes)))
                self.regions.append(((row, rows), (lane + own * lanes, lanes)))
            else:
                rows = rows // 2
                self.others.append(((row + (1 - own) * rows, rows), (lane, lanes)))
                self.regions.append(((row + own * rows, rows), (lane, lanes)))
        self.steps = len(order) + self.halvings
        self.copies = {}

    def view(self, buffer, region):
        (row, rows), (lane, lanes) = region
        row = row if isinstance(row, int) else pl.multiple_of(row, 16 if self.buffer.dtype == bf16 else 8)
        lane = lane if isinstance(lane, int) else pl.multiple_of(lane, 128)
        return buffer.at[pl.ds(row, rows), pl.ds(lane, lanes)]

    def start(self, step):
        if step >= self.steps:
            return
        if step < len(self.order):
            _, target = partner_of(*self.order[step])
            region = self.others[step] if step < self.halvings else self.regions[-1]
            source, sink = self.view(self.buffer, region), self.received[step]
        else:
            back = self.halvings - 1 - (step - len(self.order))
            _, target = partner_of(*self.order[back])
            source = sink = self.view(self.gathered, self.regions[back + 1])
        copy = pltpu.make_async_remote_copy(
            src_ref=source,
            dst_ref=sink,
            send_sem=self.send.at[step],
            recv_sem=self.receive.at[step],
            device_id=target,
            device_id_type=MESH,
        )
        copy.start()
        self.copies[step] = copy

    def finish(self, step):
        if step < 0 or step >= self.steps:
            return
        self.copies[step].wait()
        if step < len(self.order):
            region = self.regions[min(step + 1, self.halvings)]
            mine = self.view(self.buffer, region)
            result = mine if step < len(self.order) - 1 else self.view(self.gathered, region)
            result[...] = (mine[...].astype(f32) + self.received[step][...].astype(f32)).astype(mine.dtype)


def received_shapes(shape, dtype, count, lanes_first):
    rows, lanes = shape
    shapes = []
    for step in range(count):
        if step < HALVINGS:
            if step == 0 and lanes_first:
                lanes = lanes // 2
            else:
                rows = rows // 2
        shapes.append(pltpu.VMEM((rows, lanes), dtype))
    return shapes


def greet(n_wide, n_narrow):
    barrier = pltpu.get_barrier_semaphore()
    order = bits_of(n_wide, n_narrow)
    for axis, bit in order:
        pl.semaphore_signal(barrier, inc=1, device_id=partner_of(axis, bit)[1], device_id_type=MESH)
    pl.semaphore_wait(barrier, len(order))


def orders_of(n_wide, n_narrow, count):
    bits = bits_of(n_wide, n_narrow)
    middle = bits[1:-1]
    orders = []
    for index in range(count):
        turn = index % max(1, len(middle))
        orders.append(bits[:1] + middle[turn:] + middle[:turn] + bits[-1:])
    return orders


def reduce_kernel(n_wide, n_narrow, parts, *refs):
    count = len(bits_of(n_wide, n_narrow))
    ins, refs = refs[:parts], refs[parts:]
    outs, refs = refs[:parts], refs[parts:]
    buffers, refs = refs[:parts], refs[parts:]
    gathered, refs = refs[:parts], refs[parts:]
    received, refs = refs[: parts * count], refs[parts * count :]
    send, receive = refs
    greet(n_wide, n_narrow)
    orders = orders_of(n_wide, n_narrow, parts)
    works = []
    for part in range(parts):
        buffers[part][...] = ins[part][...].astype(buffers[part].dtype)
        works.append(
            Reduction(
                buffers[part],
                gathered[part],
                received[part * count : (part + 1) * count],
                send.at[part],
                receive.at[part],
                orders[part],
                buffers[part].shape[1] >= 256,
            )
        )
        works[-1].start(0)
    for step in range(1, works[0].steps + 1):
        for work in works:
            work.finish(step - 1)
            work.start(step)
    for part in range(parts):
        outs[part][...] = gathered[part][...]


def reduce_all(n_wide, n_narrow, arrays):
    parts, count = len(arrays), len(bits_of(n_wide, n_narrow))
    types = [bf16 if array.shape[1] >= 256 else f32 for array in arrays]
    scratch = [pltpu.VMEM(array.shape, kind) for array, kind in zip(arrays, types)] * 2
    for array, kind in zip(arrays, types):
        scratch += received_shapes(array.shape, kind, count, array.shape[1] >= 256)
    steps = count + min(HALVINGS, count)
    return pl.pallas_call(
        functools.partial(reduce_kernel, n_wide, n_narrow, parts),
        out_shape=[jax.ShapeDtypeStruct(array.shape, kind) for array, kind in zip(arrays, types)],
        in_specs=[pl.BlockSpec(memory_space=pltpu.VMEM)] * parts,
        out_specs=[pl.BlockSpec(memory_space=pltpu.VMEM)] * parts,
        scratch_shapes=scratch + [pltpu.SemaphoreType.DMA((parts, steps)), pltpu.SemaphoreType.DMA((parts, steps))],
        compiler_params=pltpu.CompilerParams(
            collective_id=0, has_side_effects=True, vmem_limit_bytes=VMEM_LIMIT
        ),
    )(*arrays)


def norm_back(values, gain, upstream):
    factor = lax.rsqrt(jnp.mean(values * values, axis=-1, keepdims=True) + EPSILON)
    plain = values * factor
    scaled = upstream * gain
    inner = jnp.mean(scaled * plain, axis=-1, keepdims=True)
    return factor * (scaled - plain * inner), jnp.sum(upstream * plain, axis=0)


def local(
    tokens,
    gain_one,
    w_query,
    w_key,
    w_value,
    w_out,
    table,
    gain_two,
    w_router,
    w_up,
    w_down,
    routes,
    cotangent,
):
    count, width = tokens.shape
    experts = w_router.shape[1]
    n_wide, n_narrow = lax.axis_size("wide"), lax.axis_size("narrow")
    me = lax.axis_index("wide") * n_narrow + lax.axis_index("narrow")
    capacity = max(2, (5 * count + 4 * experts - 1) // (4 * experts))
    total = experts * capacity
    sequences = count // SEQ_LEN
    groups = HEADS // GROUP
    params = pltpu.CompilerParams(vmem_limit_bytes=VMEM_LIMIT)
    buckets = jnp.asarray(lane_buckets())
    shape = jax.ShapeDtypeStruct

    target_column, target_row, sent_upstream = pl.pallas_call(
        functools.partial(slots_kernel, capacity),
        out_shape=[shape((count, 1), jnp.int32), shape((1, count), jnp.int32), shape((total, width), bf16)],
        compiler_params=params,
        name="slots",
    )(routes, routes.reshape(1, count), cotangent)

    def exchange(rows):
        return lax.all_to_all(rows.reshape(experts, capacity, width), BOTH, 0, 0, tiled=True).reshape(total, width)

    upstream_rows = exchange(sent_upstream)

    columns = pl.BlockSpec((count, COLUMNS), lambda g: (0, g))
    rows_t = pl.BlockSpec((COLUMNS, count), lambda g: (g, 0))
    weight = pl.BlockSpec((width, COLUMNS), lambda g: (0, g))
    weights_block = pl.BlockSpec((GROUP, sequences, SEQ_LEN, SEQ_LEN), lambda g: (g, 0, 0, 0))
    (
        hidden,
        normed_one,
        normed_t,
        query,
        key_t,
        value,
        weights,
        mixed_t,
        normed_two,
        probs,
        gate,
        sent_rows,
    ) = pl.pallas_call(
        functools.partial(forward_kernel, capacity),
        grid=(groups,),
        in_specs=[
            whole((count, width)),
            whole((1, width)),
            weight,
            weight,
            weight,
            pl.BlockSpec((COLUMNS, width), lambda g: (g, 0)),
            whole((BUCKETS, HEADS)),
            whole((SPAN, BUCKETS)),
            pl.BlockSpec(memory_space=pltpu.SMEM),
            whole((1, width)),
            whole((width, experts)),
            whole((count, 1)),
            whole((1, count)),
        ],
        out_specs=[
            whole((count, width)),
            whole((count, width)),
            whole((width, count)),
            columns,
            rows_t,
            columns,
            weights_block,
            rows_t,
            whole((count, width)),
            whole((count, experts)),
            whole((count, 1)),
            whole((total, width)),
        ],
        out_shape=[
            shape((count, width), f32),
            shape((count, width), bf16),
            shape((width, count), bf16),
            shape((count, width), bf16),
            shape((width, count), bf16),
            shape((count, width), bf16),
            shape((HEADS, sequences, SEQ_LEN, SEQ_LEN), bf16),
            shape((width, count), bf16),
            shape((count, width), bf16),
            shape((count, experts), f32),
            shape((count, 1), f32),
            shape((total, width), bf16),
        ],
        scratch_shapes=[
            pltpu.VMEM((HEADS, TILE, SPAN), f32),
            pltpu.VMEM((count, COLUMNS), bf16),
            pltpu.VMEM((COLUMNS, count), bf16),
            pltpu.VMEM((COLUMNS, count), bf16),
        ],
        compiler_params=params,
        cost_estimate=pl.CostEstimate(flops=14 * 10**9, bytes_accessed=40 * 10**6, transcendentals=10**7),
        name="attention_forward",
    )(
        tokens,
        gain_one[None],
        w_query,
        w_key,
        w_value,
        w_out,
        table,
        buckets,
        table,
        gain_two[None],
        w_router,
        routes,
        target_row,
    )

    rows = exchange(sent_rows)
    logits = product(rows, w_router)
    rows_probs = jax.nn.softmax(logits, axis=-1)
    rows_gate = jnp.sum(jnp.where(jnp.arange(experts)[None, :] == me, rows_probs, 0.0), axis=1, keepdims=True)
    arrived_bar = (rows_gate * upstream_rows.astype(f32)).astype(bf16)
    raised = product(rows, w_up[0])
    active, gelu_pull = jax.vjp(gelu_curve, raised)
    active = active.astype(bf16)
    produced = product(active, w_down[0]).astype(bf16)
    returned = exchange(produced)
    active_bar = product_right(arrived_bar, w_down[0])
    raised_bar = gelu_pull(active_bar)[0].astype(bf16)
    rows_bar = product_right(raised_bar, w_up[0]).astype(bf16)
    returned_bar = exchange(rows_bar)
    down_grad = product_left(active, arrived_bar)
    up_grad = product_left(rows, raised_bar)

    placing = (target_column == jnp.arange(total, dtype=jnp.int32)[None, :]).astype(bf16)
    gathered = product(placing, returned)
    output = (hidden + gate * gathered).astype(bf16)
    upstream = cotangent.astype(f32)
    gate_bar = jnp.sum(upstream * gathered, axis=-1, keepdims=True)
    picks = routes == jnp.arange(experts, dtype=jnp.int32)[None, :]
    logits_bar = (probs * (jnp.where(picks, gate_bar, 0.0) - gate * gate_bar)).astype(bf16)
    normed_two_bar = product(placing, returned_bar) + product_right(logits_bar, w_router)
    router_grad = product_left(normed_two, logits_bar)
    hidden_norm_bar, gain_two_grad = norm_back(hidden, gain_two, normed_two_bar)
    hidden_bar = upstream + hidden_norm_bar
    hidden_low = hidden_bar.astype(bf16)
    out_grad = product(mixed_t, hidden_low).astype(bf16)
    mixed_bar = product_right(hidden_low, w_out).astype(bf16)
    mixed_bar_t = product_right(w_out, hidden_low).astype(bf16)

    query_grad, key_grad, value_grad, normed_one_bar, table_grad = pl.pallas_call(
        backward_kernel,
        grid=(groups,),
        in_specs=[
            columns,
            rows_t,
            columns,
            rows_t,
            columns,
            weights_block,
            whole((width, count)),
            weight,
            weight,
            weight,
            whole((SPAN, BUCKETS)),
        ],
        out_specs=[weight, weight, weight, whole((count, width)), whole((16, BUCKETS))],
        out_shape=[
            shape((width, width), bf16),
            shape((width, width), bf16),
            shape((width, width), bf16),
            shape((count, width), f32),
            shape((16, BUCKETS), f32),
        ],
        scratch_shapes=[
            pltpu.VMEM((SEQ_LEN, SEQ_LEN), bf16),
            pltpu.VMEM((COLUMNS, count), bf16),
            pltpu.VMEM((count, COLUMNS), bf16),
            pltpu.VMEM((count, COLUMNS), bf16),
            pltpu.VMEM((TILE, SPAN), f32),
            pltpu.VMEM((2, 8, TILE), f32),
            pltpu.VMEM((16, SPAN), f32),
        ],
        compiler_params=params,
        cost_estimate=pl.CostEstimate(flops=20 * 10**9, bytes_accessed=40 * 10**6, transcendentals=0),
        name="attention_backward",
    )(
        mixed_bar,
        mixed_bar_t,
        query,
        key_t,
        value,
        weights,
        normed_t,
        w_query,
        w_key,
        w_value,
        buckets,
    )
    inputs = tokens.astype(f32)
    inputs_norm_bar, gain_one_grad = norm_back(inputs, gain_one, normed_one_bar)
    tokens_grad = (hidden_bar + inputs_norm_bar).astype(bf16)

    small = [gain_one_grad, gain_two_grad, table_grad[:HEADS].reshape(-1), router_grad.reshape(-1)]
    sizes = [part.size for part in small]
    length = -(-sum(sizes) // (256 * 128)) * 256 * 128
    packed = jnp.concatenate(small + [jnp.zeros((length - sum(sizes),), f32)]).reshape(-1, 128)
    out_grad, query_grad, key_grad, value_grad, packed = reduce_all(
        n_wide, n_narrow, [out_grad, query_grad, key_grad, value_grad, packed]
    )
    packed = packed.reshape(-1)
    ends = np.cumsum(sizes)
    gain_one_grad = packed[: ends[0]]
    gain_two_grad = packed[ends[0] : ends[1]]
    table_grad = packed[ends[1] : ends[2]].reshape(HEADS, BUCKETS).T
    router_grad = packed[ends[2] : ends[3]].reshape(width, experts)
    return (
        output,
        tokens_grad,
        gain_one_grad,
        query_grad.astype(f32),
        key_grad.astype(f32),
        value_grad.astype(f32),
        out_grad.astype(f32),
        table_grad,
        gain_two_grad,
        router_grad,
        up_grad[None],
        down_grad[None],
    )


def solution(mesh):
    split = P(BOTH, None)
    experts = P(BOTH, None, None)
    in_specs = (split, P(), P(), P(), P(), P(), P(), P(), P(), experts, experts, split, split)
    out_specs = (split, split, P(), P(), P(), P(), P(), P(), P(), P(), experts, experts)
    return jax.shard_map(local, mesh=mesh, in_specs=in_specs, out_specs=out_specs, check_vma=False)
```

```python
import functools

import jax
import jax.numpy as jnp
import numpy as np
from jax import lax
from jax.experimental import pallas as pl
from jax.experimental.pallas import tpu as pltpu
from jax.sharding import PartitionSpec as P

HEADS = 12
HEAD_DIM = 64
BUCKETS = 32
SEQ_LEN = 512
EPSILON = 1e-06
LIMITS = (12, 16, 23, 32, 46, 64, 91)
HIGHEST = lax.Precision.HIGHEST
MESH = pl.DeviceIdType.MESH
BOTH = ("wide", "narrow")
GROUP = 4
COLUMNS = GROUP * HEAD_DIM
TILE = 128
SPAN = 512
HALF = 256
PIECE = 256
VMEM_LIMIT = 56 * 2**20

bf16 = jnp.bfloat16
f32 = jnp.float32


def product(left, right, **options):
    return jnp.dot(left, right, preferred_element_type=f32, **options)


def product_left(left, right, **options):
    return lax.dot_general(left, right, (((0,), (0,)), ((), ())), preferred_element_type=f32, **options)


def product_right(left, right, **options):
    return lax.dot_general(left, right, (((1,), (1,)), ((), ())), preferred_element_type=f32, **options)


def gelu_curve(values):
    return jax.nn.gelu(values, approximate=True)


def lane_buckets():
    offset = SPAN // 2 - np.arange(SPAN)
    distance = np.abs(offset)
    further = 8 + sum((distance >= limit).astype(np.int32) for limit in LIMITS)
    bucket = np.where(distance < 8, distance, further) + 16 * (offset > 0)
    return (bucket[:, None] == np.arange(BUCKETS)[None, :]).astype(np.float32)


def whole(shape):
    return pl.BlockSpec(shape, lambda *_: (0,) * len(shape))


def slots_kernel(capacity, column_ref, row_ref, rows_ref, target_column_ref, target_row_ref, sent_ref):
    count = column_ref.shape[0]
    experts = sent_ref.shape[0] // capacity
    token_down = lax.broadcasted_iota(jnp.int32, (count, count), 0)
    token_across = lax.broadcasted_iota(jnp.int32, (count, count), 1)
    column = column_ref[...]
    picks = column == lax.broadcasted_iota(jnp.int32, (count, experts), 1)
    earlier = (token_down > token_across).astype(bf16)
    before = product(earlier, picks.astype(bf16))
    slot = jnp.sum(jnp.where(picks, before, 0.0), axis=1, keepdims=True).astype(jnp.int32)
    target_column_ref[...] = jnp.where(slot < capacity, column * capacity + slot, -1)
    row = row_ref[...]
    picks = row == lax.broadcasted_iota(jnp.int32, (experts, count), 0)
    earlier = (token_down < token_across).astype(bf16)
    before = product(picks.astype(bf16), earlier)
    slot = jnp.sum(jnp.where(picks, before, 0.0), axis=0, keepdims=True).astype(jnp.int32)
    target = jnp.where(slot < capacity, row * capacity + slot, -1)
    target_row_ref[...] = target
    place_rows(target, rows_ref, sent_ref)


def place_rows(target, rows_ref, sent_ref):
    total, count = sent_ref.shape[0], rows_ref.shape[0]
    piece = total // 4

    def body(index, carry):
        start = pl.multiple_of(index * piece, 16)
        slots = start + lax.broadcasted_iota(jnp.int32, (piece, count), 0)
        placing = (slots == target).astype(bf16)
        sent_ref[pl.ds(start, piece), :] = product(placing, rows_ref[...]).astype(bf16)
        return carry

    lax.fori_loop(0, total // piece, body, 0)


def forward_kernel(
    capacity,
    tokens_ref,
    gain_one_ref,
    w_query_ref,
    w_key_ref,
    w_value_ref,
    w_out_ref,
    table_ref,
    buckets_ref,
    far_ref,
    gain_two_ref,
    w_router_ref,
    column_ref,
    target_ref,
    hidden_ref,
    normed_ref,
    normed_t_ref,
    query_ref,
    key_t_ref,
    value_ref,
    weights_ref,
    mixed_t_ref,
    normed_two_ref,
    probs_ref,
    gate_ref,
    sent_ref,
    curves,
    key_rows,
    query_t,
    value_t,
):
    group = pl.program_id(0)
    count, width = tokens_ref.shape
    sequences = count // SEQ_LEN

    @pl.when(group == 0)
    def _():
        inputs = tokens_ref[...].astype(f32)
        factor = lax.rsqrt(jnp.mean(inputs * inputs, axis=1, keepdims=True) + EPSILON)
        normed = (inputs * factor * gain_one_ref[...]).astype(bf16)
        normed_ref[...] = normed
        normed_t_ref[...] = normed.T
        hidden_ref[...] = inputs
        curve = lax.dot_general(
            table_ref[...], buckets_ref[...], (((0,), (1,)), ((), ())), preferred_element_type=f32, precision=HIGHEST
        )
        for head in range(HEADS):
            wide = jnp.broadcast_to(curve[head : head + 1, :], (TILE, SPAN))
            curves[head] = pltpu.roll(wide, 0, 1, stride=1, stride_axis=0)

    normed = normed_ref[...]
    query = product(normed, w_query_ref[...]).astype(bf16)
    query_ref[...] = query
    query_t[...] = (query * jnp.asarray(HEAD_DIM**-0.5, bf16)).T
    key = product(normed, w_key_ref[...]).astype(bf16)
    key_rows[...] = key
    key_t_ref[...] = key.T
    value = product(normed, w_value_ref[...]).astype(bf16)
    value_ref[...] = value
    value_t[...] = value.T

    lane = lax.broadcasted_iota(jnp.int32, (SEQ_LEN, TILE), 1)
    for head in range(GROUP):
        pair = head // 2 * TILE
        mine = (lane // HEAD_DIM) == head % 2
        index = group * GROUP + head
        far_left = far_ref[15, index]
        far_right = far_ref[31, index]
        for sequence in range(sequences):
            rows = pl.ds(sequence * SEQ_LEN, SEQ_LEN)
            keys = jnp.where(mine, key_rows[rows, pair : pair + TILE], jnp.zeros((), bf16))
            for half in range(SEQ_LEN // HALF):
                columns = pl.ds(sequence * SEQ_LEN + half * HALF, HALF)
                raw = product(keys, query_t[pair : pair + TILE, columns])
                parts = []
                for down in range(SEQ_LEN // TILE):
                    line = []
                    for across in range(HALF // TILE):
                        step = down - (half * (HALF // TILE) + across)
                        block = raw[down * TILE : (down + 1) * TILE, across * TILE : (across + 1) * TILE]
                        if abs(step) <= 1:
                            begin = SPAN // 2 - step * TILE
                            bias = curves[index, :, begin : begin + TILE]
                        else:
                            bias = far_right if step > 0 else far_left
                        line.append(block + bias)
                    parts.append(jnp.concatenate(line, axis=1))
                scores = jnp.concatenate(parts, axis=0)
                maximum = jnp.max(scores, axis=0, keepdims=True)
                exponent = jnp.exp(scores - maximum)
                total = jnp.sum(exponent, axis=0, keepdims=True)
                weights = (exponent * (1.0 / total)).astype(bf16)
                weights_ref[head, sequence, :, half * HALF : (half + 1) * HALF] = weights
                mixed_t_ref[head * HEAD_DIM : (head + 1) * HEAD_DIM, columns] = product(
                    value_t[head * HEAD_DIM : (head + 1) * HEAD_DIM, rows], weights
                ).astype(bf16)
    hidden_ref[...] += product(mixed_t_ref[...].T, w_out_ref[...])

    @pl.when(group == pl.num_programs(0) - 1)
    def _():
        hidden = hidden_ref[...]
        factor = lax.rsqrt(jnp.mean(hidden * hidden, axis=1, keepdims=True) + EPSILON)
        normed_two = (hidden * factor * gain_two_ref[...]).astype(bf16)
        normed_two_ref[...] = normed_two
        logits = product(normed_two, w_router_ref[...])
        exponent = jnp.exp(logits - jnp.max(logits, axis=1, keepdims=True))
        probs = exponent / jnp.sum(exponent, axis=1, keepdims=True)
        probs_ref[...] = probs
        picks = column_ref[...] == lax.broadcasted_iota(jnp.int32, probs.shape, 1)
        gate_ref[...] = jnp.sum(jnp.where(picks, probs, 0.0), axis=1, keepdims=True)
        place_rows(target_ref[...], normed_two_ref, sent_ref)


def norm_back(values, gain, upstream):
    factor = lax.rsqrt(jnp.mean(values * values, axis=-1, keepdims=True) + EPSILON)
    plain = values * factor
    scaled = upstream * gain
    inner = jnp.mean(scaled * plain, axis=-1, keepdims=True)
    return factor * (scaled - plain * inner), jnp.sum(upstream * plain, axis=0, keepdims=True)


def small_rows(experts):
    return experts, experts + 16, experts + 17, -(-(experts + 18) // 64) * 64


def backward_kernel(
    n_wide,
    n_narrow,
    groups,
    produced_ref,
    returned_bar_ref,
    gate_lines_ref,
    target_ref,
    column_ref,
    hidden_ref,
    cotangent_ref,
    probs_ref,
    gate_ref,
    gain_two_ref,
    w_router_ref,
    mixed_t_ref,
    w_out_ref,
    tokens_ref,
    gain_one_ref,
    query_ref,
    key_t_ref,
    value_ref,
    weights_ref,
    normed_t_ref,
    w_query_ref,
    w_key_ref,
    w_value_ref,
    buckets_ref,
    *refs,
):
    parts = groups + 2
    bits = len(bits_of(n_wide, n_narrow))
    returned_ref, result_ref, refs = refs[0], refs[1], refs[2:]
    outs, refs = refs[:parts], refs[parts:]
    buffers, refs = refs[:parts], refs[parts:]
    sums, refs = refs[:parts], refs[parts:]
    received, refs = refs[: parts * bits], refs[parts * bits :]
    (
        hidden_bar,
        tokens_grad_ref,
        mixed_bar,
        mixed_bar_t,
        normed_bar,
        scores_s,
        query_bar_t,
        query_rows,
        key_bar,
        value_bar,
        near,
        far,
        diagonals,
        send,
        receive,
        back_send,
        back_receive,
        own_sems,
    ) = refs
    hidden_low = tokens_grad_ref
    group = pl.program_id(0)
    count, width = normed_bar.shape
    experts, capacity = produced_ref.shape[:2]
    total = experts * capacity
    sequences = count // SEQ_LEN
    scale = HEAD_DIM**-0.5
    net = Exchange(n_wide, n_narrow)
    router_end, gain_two_at, gain_one_at, _ = small_rows(experts)
    orders = orders_of(n_wide, n_narrow, parts)
    works = []
    for part in range(parts):
        works.append(
            Reduction(
                buffers[part],
                sums[part],
                received[part * bits : (part + 1) * bits],
                send.at[part],
                receive.at[part],
                orders[part],
                min(bits, 4 if part == parts - 1 else 5),
                True,
            )
        )
    own_copy = pltpu.make_async_copy(produced_ref.at[net.place], returned_ref.at[net.me], own_sems.at[0])
    hidden_copy = pltpu.make_async_copy(hidden_ref, hidden_bar, own_sems.at[1])
    cotangent_copy = pltpu.make_async_copy(cotangent_ref, tokens_grad_ref, own_sems.at[2])
    tokens_copy = pltpu.make_async_copy(tokens_ref, mixed_bar, own_sems.at[3])
    small = buffers[-1]

    @pl.when(group == 0)
    def _():
        hidden_copy.start()
        cotangent_copy.start()
        net.greet()
        for part in ISSUE:
            if part < net.parts:
                net.start_back(produced_ref, returned_ref, back_send, back_receive, part)
        own_copy.start()
        diagonals[...] = jnp.zeros_like(diagonals)
        small[...] = jnp.zeros_like(small)
        hidden_copy.wait()
        cotangent_copy.wait()

        def prologue(index, carry):
            rows = pl.ds(pl.multiple_of(index * PIECE, PIECE), PIECE)
            target = target_ref[rows, :]
            chosen = column_ref[rows, :]
            placing = (target == lax.broadcasted_iota(jnp.int32, (PIECE, total), 1)).astype(bf16)
            normed_two_bar = product(placing, returned_bar_ref[...])
            picks = chosen == lax.broadcasted_iota(jnp.int32, (PIECE, experts), 1)
            lines = product(picks.astype(f32), gate_lines_ref[...], precision=HIGHEST)
            slots = (target - chosen * capacity) == lax.broadcasted_iota(jnp.int32, (PIECE, 128), 1)
            gate_bar = jnp.sum(jnp.where(slots, lines, 0.0), axis=1, keepdims=True)
            inner = gate_ref[rows, :] * gate_bar
            logits_bar = (probs_ref[rows, :] * (jnp.where(picks, gate_bar, 0.0) - inner)).astype(bf16)
            normed_two_bar = normed_two_bar + product_right(logits_bar, w_router_ref[...])
            hidden = hidden_bar[rows, :]
            factor = lax.rsqrt(jnp.mean(hidden * hidden, axis=1, keepdims=True) + EPSILON)
            normed_two = (hidden * factor * gain_two_ref[...]).astype(bf16)
            small[0:router_end, :] += product_left(logits_bar, normed_two)
            back, gain_part = norm_back(hidden, gain_two_ref[...], normed_two_bar)
            small[gain_two_at : gain_two_at + 1, :] += gain_part
            bar = tokens_grad_ref[rows, :].astype(f32) + back
            hidden_bar[rows, :] = bar
            low = bar.astype(bf16)
            hidden_low[rows, :] = low
            mixed_bar[rows, :] = product_right(low, w_out_ref[...]).astype(bf16)
            return carry

        lax.fori_loop(0, count // PIECE, prologue, 0)
        buffers[0][...] = product(mixed_t_ref[...], hidden_low[...]).astype(bf16)
        works[0].start(0)
        mixed_bar_t[...] = product_right(w_out_ref[...], hidden_low[...]).astype(bf16)

    def tick(head):
        for now in range(groups):
            active = [(0, now * GROUP + head)] + [
                (part, (now - part) * GROUP + head) for part in range(1, now + 1)
            ]

            @pl.when(group == now)
            def _(active=active):
                for part, step in active:
                    works[part].finish(step)
                    works[part].start(step + 1)

    lane = lax.broadcasted_iota(jnp.int32, (SEQ_LEN, TILE), 1)
    features = pl.ds(pl.multiple_of(group * COLUMNS, COLUMNS), COLUMNS)
    for head in range(GROUP):
        pair = pl.ds(pl.multiple_of(group * COLUMNS + head // 2 * TILE, TILE), TILE)
        local_pair = pl.ds(head // 2 * TILE, TILE)
        mine = (lane // HEAD_DIM) == head % 2
        feature = pl.ds(head * HEAD_DIM, HEAD_DIM)
        near[...] = jnp.zeros_like(near)
        far[...] = jnp.zeros_like(far)
        for sequence in range(sequences):
            rows = pl.ds(sequence * SEQ_LEN, SEQ_LEN)
            values = jnp.where(mine, value_ref[rows, local_pair], jnp.zeros((), bf16))
            for half in range(SEQ_LEN // HALF):
                columns = pl.ds(sequence * SEQ_LEN + half * HALF, HALF)
                probs_bar = product(values, mixed_bar_t[pair, columns])
                probs = weights_ref[head, sequence, :, half * HALF : (half + 1) * HALF].astype(f32)
                shared = probs * probs_bar
                summed = jnp.sum(shared, axis=0, keepdims=True)
                scores_bar = shared - probs * summed
                scores_s[:, half * HALF : (half + 1) * HALF] = scores_bar.astype(bf16)
                for down in range(SEQ_LEN // TILE):
                    for across in range(HALF // TILE):
                        step = down - (half * (HALF // TILE) + across)
                        block = scores_bar[down * TILE : (down + 1) * TILE, across * TILE : (across + 1) * TILE]
                        if abs(step) <= 1:
                            begin = SPAN // 2 - step * TILE
                            near[:, begin : begin + TILE] += block
                        else:
                            side = 1 if step > 0 else 0
                            far[side] += jnp.sum(block.reshape(TILE // 8, 8, TILE), axis=0)
            weights = weights_ref[head, sequence]
            scores_low = scores_s[...]
            value_part = product(weights, mixed_bar[rows, pair]).astype(bf16)
            key_part = (product(scores_low, query_ref[rows, local_pair]) * scale).astype(bf16)
            if head % 2 == 0:
                value_bar[rows, local_pair] = value_part
                key_bar[rows, local_pair] = key_part
            else:
                value_bar[rows, local_pair] = jnp.where(mine, value_part, value_bar[rows, local_pair])
                key_bar[rows, local_pair] = jnp.where(mine, key_part, key_bar[rows, local_pair])
            query_bar_t[feature, rows] = (product(key_t_ref[feature, rows], scores_low) * scale).astype(bf16)
        folded = near[0:8, :]
        for step in range(1, TILE // 8):
            folded = folded + pltpu.roll(near[8 * step : 8 * step + 8, :], SPAN - 8 * step, 1)
        place = lax.broadcasted_iota(jnp.int32, (8, SPAN), 0)
        for bit in (4, 2, 1):
            folded = jnp.where((place & bit) > 0, pltpu.roll(folded, SPAN - bit, 1), folded)
        gathered = jnp.sum(folded, axis=0, keepdims=True)
        place = lax.broadcasted_iota(jnp.int32, (1, SPAN), 1)
        left = jnp.sum(far[0])
        right = jnp.sum(far[1])
        gathered = gathered + jnp.where(place == SPAN - 1, left, 0.0) + jnp.where(place == 0, right, 0.0)
        diagonals[pl.ds(group * GROUP + head, 1), :] = gathered
        tick(head)

    @pl.when(group == groups - 1)
    def _():
        tokens_copy.start()

    query_bar = query_bar_t[...].T
    normed_t = normed_t_ref[...]
    grads = [product(normed_t, part).astype(bf16) for part in (query_bar, key_bar[...], value_bar[...])]
    for now in range(groups):

        @pl.when(group == now)
        def _(now=now):
            for index, grad in enumerate(grads):
                buffers[now + 1][:, index * COLUMNS : (index + 1) * COLUMNS] = grad
            works[now + 1].start(0)

    query_rows[...] = query_bar

    def project(index, carry):
        rows = pl.ds(pl.multiple_of(index * PIECE, PIECE), PIECE)
        bar = (
            product_right(query_rows[rows, :], w_query_ref[...])
            + product_right(key_bar[rows, :], w_key_ref[...])
            + product_right(value_bar[rows, :], w_value_ref[...])
        )

        @pl.when(group == 0)
        def _():
            normed_bar[rows, :] = bar

        @pl.when(group > 0)
        def _():
            normed_bar[rows, :] += bar

        @pl.when(group == groups - 1)
        def _():
            back, gain_part = norm_back(mixed_bar[rows, :].astype(f32), gain_one_ref[...], normed_bar[rows, :])
            tokens_grad_ref[rows, :] = (hidden_bar[rows, :] + back).astype(bf16)
            small[gain_one_at : gain_one_at + 1, :] += gain_part

        return carry

    @pl.when(group == groups - 1)
    def _():
        tokens_copy.wait()

    lax.fori_loop(0, count // PIECE, project, 0)

    @pl.when(group == groups - 1)
    def _():
        small[router_end : router_end + 16, 0:BUCKETS] = product(
            diagonals[...], buckets_ref[...], precision=HIGHEST
        )
        works[-1].start(0)
        at = [groups * GROUP] + [(groups - part) * GROUP for part in range(1, groups + 1)] + [0]
        while any(step < work.steps for step, work in zip(at, works)):
            for part, work in enumerate(works):
                work.finish(at[part])
                work.start(at[part] + 1)
                at[part] += 1
        outward = [pltpu.make_async_copy(tokens_grad_ref, result_ref, own_sems.at[4])]
        outward += [pltpu.make_async_copy(sums[part], outs[part], own_sems.at[5 + part]) for part in range(parts)]
        for copy in outward:
            copy.start()
        for copy in outward:
            copy.wait()
        own_copy.wait()
        for part in range(net.parts):
            net.wait_back(produced_ref, returned_ref, back_send, back_receive, part)
        net.wait_returns(returned_ref, back_send, back_receive)


def partner_of(axis, bit):
    w, k = lax.axis_index("wide"), lax.axis_index("narrow")
    place = w if axis == "wide" else k
    own = (place // bit) % 2
    other = place + bit - 2 * bit * own
    return own, ((other, k) if axis == "wide" else (w, other))


def bits_of(n_wide, n_narrow):
    narrow = [("narrow", 1 << b) for b in range(n_narrow.bit_length() - 1)]
    wide = [("wide", 1 << b) for b in range(n_wide.bit_length() - 1)]
    return narrow + wide


class Reduction:
    def __init__(self, buffer, gathered, received, send, receive, order, halvings, lanes_first):
        self.buffer, self.gathered, self.received = buffer, gathered, received
        self.send, self.receive = send, receive
        self.order, self.halvings = order, halvings
        self.own = [partner_of(*bit) for bit in order]
        rows, lanes = buffer.shape
        self.regions = [((0, rows), (0, lanes))]
        self.others = []
        for step in range(self.halvings):
            own, _ = self.own[step]
            (row, rows), (lane, lanes) = self.regions[-1]
            if step == 0 and lanes_first:
                lanes = lanes // 2
                self.others.append(((row, rows), (lane + (1 - own) * lanes, lanes)))
                self.regions.append(((row, rows), (lane + own * lanes, lanes)))
            else:
                rows = rows // 2
                self.others.append(((row + (1 - own) * rows, rows), (lane, lanes)))
                self.regions.append(((row + own * rows, rows), (lane, lanes)))
        self.steps = len(order) + self.halvings

    def view(self, buffer, region):
        (row, rows), (lane, lanes) = region
        row = row if isinstance(row, int) else pl.multiple_of(row, 16 if self.buffer.dtype == bf16 else 8)
        lane = lane if isinstance(lane, int) else pl.multiple_of(lane, 128)
        return buffer.at[pl.ds(row, rows), pl.ds(lane, lanes)]

    def copy(self, step):
        if step < len(self.order):
            target = self.own[step][1]
            region = self.others[step] if step < self.halvings else self.regions[-1]
            source, sink = self.view(self.buffer, region), self.received[step]
        else:
            back = self.halvings - 1 - (step - len(self.order))
            target = self.own[back][1]
            source = sink = self.view(self.gathered, self.regions[back + 1])
        return pltpu.make_async_remote_copy(
            src_ref=source,
            dst_ref=sink,
            send_sem=self.send.at[step],
            recv_sem=self.receive.at[step],
            device_id=target,
            device_id_type=MESH,
        )

    def start(self, step):
        if 0 <= step < self.steps:
            self.copy(step).start()

    def finish(self, step):
        if not 0 <= step < self.steps:
            return
        self.copy(step).wait()
        if step < len(self.order):
            region = self.regions[min(step + 1, self.halvings)]
            mine = self.view(self.buffer, region)
            result = mine if step < len(self.order) - 1 else self.view(self.gathered, region)
            result[...] = (mine[...].astype(f32) + self.received[step][...].astype(f32)).astype(mine.dtype)


def received_shapes(shape, dtype, count, halvings, lanes_first):
    rows, lanes = shape
    shapes = []
    for step in range(count):
        if step < halvings:
            if step == 0 and lanes_first:
                lanes = lanes // 2
            else:
                rows = rows // 2
        shapes.append(pltpu.VMEM((rows, lanes), dtype))
    return shapes


def orders_of(n_wide, n_narrow, count):
    bits = bits_of(n_wide, n_narrow)
    middle = bits[1:-1]
    orders = []
    for index in range(count):
        turn = index % max(1, len(middle))
        orders.append(bits[:1] + middle[turn:] + middle[:turn] + bits[-1:])
    return orders


class Exchange:
    def __init__(self, n_wide, n_narrow):
        self.n_wide, self.n_narrow = n_wide, n_narrow
        self.count = n_wide * n_narrow
        self.parts = min(4, n_wide)
        self.rows = n_wide // self.parts
        self.length = self.rows * n_narrow
        w, k = lax.axis_index("wide"), lax.axis_index("narrow")
        self.me = w * n_narrow + k
        self.top, self.place = w // self.rows, (w % self.rows) * n_narrow + k

    def partner(self, part, place):
        top, bit = self.top, 1
        while bit < self.parts:
            if part & bit:
                top = top + bit - 2 * bit * ((top // bit) % 2)
            bit *= 2
        w = top * self.rows + place // self.n_narrow
        return w, place % self.n_narrow

    def each(self, part, act):
        def body(place, carry):
            if part == 0:

                @pl.when(place != self.place)
                def _():
                    act(place)

            else:
                act(place)
            return carry

        lax.fori_loop(0, self.length, body, 0)

    def greet(self):
        barrier = pltpu.get_barrier_semaphore()
        for part in range(self.parts):

            def act(place, part=part):
                pl.semaphore_signal(barrier, inc=1, device_id=self.partner(part, place), device_id_type=MESH)

            self.each(part, act)
        pl.semaphore_wait(barrier, self.count - 1)

    def out(self, source, sink, send, receive, part, place):
        w, k = self.partner(part, place)
        slot = part * self.length
        return pltpu.make_async_remote_copy(
            src_ref=source.at[w * self.n_narrow + k],
            dst_ref=sink.at[slot + self.place],
            send_sem=send.at[slot + place],
            recv_sem=receive.at[slot + self.place],
            device_id=(w, k),
            device_id_type=MESH,
        )

    def back(self, source, sink, send, receive, part, place):
        slot = part * self.length + place
        return pltpu.make_async_remote_copy(
            src_ref=source.at[slot],
            dst_ref=sink.at[self.me],
            send_sem=send.at[slot],
            recv_sem=receive.at[self.me],
            device_id=self.partner(part, place),
            device_id_type=MESH,
        )

    def arrival(self, sink, send, receive, slot):
        return pltpu.make_async_remote_copy(
            src_ref=sink.at[slot],
            dst_ref=sink.at[slot],
            send_sem=send.at[slot],
            recv_sem=receive.at[slot],
            device_id=self.partner(self.parts - 1, self.place),
            device_id_type=MESH,
        )

    def start_out(self, source, sink, send, receive, part):
        self.each(part, lambda place: self.out(source, sink, send, receive, part, place).start())

    def wait_out(self, source, sink, send, receive, part):
        self.each(part, lambda place: self.out(source, sink, send, receive, part, place).wait_send())

    def wait_arrivals(self, sink, send, receive, part):
        slot = part * self.length
        self.each(part, lambda place: self.arrival(sink, send, receive, slot + place).wait_recv())

    def start_back(self, source, sink, send, receive, part):
        self.each(part, lambda place: self.back(source, sink, send, receive, part, place).start())

    def wait_back(self, source, sink, send, receive, part):
        self.each(part, lambda place: self.back(source, sink, send, receive, part, place).wait_send())

    def wait_returns(self, sink, send, receive):
        def body(slot, carry):
            @pl.when(slot != self.me)
            def _():
                self.arrival(sink, send, receive, slot).wait_recv()

            return carry

        lax.fori_loop(0, self.count, body, 0)


ISSUE = (2, 3, 1, 0)


def experts_kernel(
    n_wide,
    n_narrow,
    sent_ref,
    upstream_ref,
    w_up_ref,
    w_down_ref,
    w_router_ref,
    back_ref,
    gate_back_ref,
    produced_ref,
    up_grad_ref,
    down_grad_ref,
    rows_s,
    upstream_s,
    w_up_s,
    w_down_s,
    active_s,
    bar_s,
    rows_bar_s,
    produced_s,
    gate_s,
    scaled_s,
    rows_t_s,
    stage_s,
    send,
    receive,
    back_send,
    back_receive,
    gate_send,
    gate_receive,
    local_sems,
):
    net = Exchange(n_wide, n_narrow)
    count, capacity, width = rows_s.shape
    length = net.length
    piece = length * capacity
    hidden_units = w_up_s.shape[1]
    tile = min(768, hidden_units)
    tiles = hidden_units // tile
    down_copy = pltpu.make_async_copy(w_down_ref, w_down_s, local_sems.at[0])
    down_copy.start()
    upstream_copy = pltpu.make_async_copy(upstream_ref, upstream_s, local_sems.at[1])
    upstream_copy.start()
    up_copy = pltpu.make_async_copy(w_up_ref, w_up_s, local_sems.at[2])
    up_copy.start()
    own_copy = pltpu.make_async_copy(sent_ref.at[net.me], rows_s.at[net.place], local_sems.at[3])
    own_copy.start()
    net.greet()
    for part in ISSUE:
        if part < net.parts:
            net.start_out(sent_ref, rows_s, send, receive, part)
    down_copy.wait()
    upstream_copy.wait()

    def before(index, carry):
        part, span = index // tiles, index % tiles
        units = pl.ds(pl.multiple_of(span * tile, tile), tile)
        upstream = upstream_s[pl.ds(part * length, length)].reshape(piece, width)
        bar_s[part, :, units] = product_right(upstream, w_down_s[units, :]).astype(bf16)
        return carry

    lax.fori_loop(0, net.parts * tiles, before, 0)
    up_copy.wait()
    own_copy.wait()
    experts = w_router_ref.shape[1]
    for part in range(net.parts):
        net.wait_arrivals(rows_s, send, receive, part)
        blocks = pl.ds(part * length, length)
        rows = rows_s[blocks].reshape(piece, width)
        upstream = upstream_s[blocks].reshape(piece, width).astype(f32)
        logits = product(rows, w_router_ref[...])
        exponent = jnp.exp(logits - jnp.max(logits, axis=1, keepdims=True))
        probs = exponent / jnp.sum(exponent, axis=1, keepdims=True)
        mine = lax.broadcasted_iota(jnp.int32, probs.shape, 1) == net.me
        gate = jnp.sum(jnp.where(mine, probs, 0.0), axis=1, keepdims=True)
        scaled_s[part * piece : (part + 1) * piece, :] = (gate * upstream).astype(bf16)

        def through(span, carry):
            produced, rows_bar = carry
            units = pl.ds(pl.multiple_of(span * tile, tile), tile)
            raised = product(rows, w_up_s[:, units])
            square = raised * raised
            inner = raised * (0.7978845608028654 + 0.7978845608028654 * 0.044715 * square)
            half = 0.5 + 0.5 * jnp.tanh(inner)
            active = (raised * half).astype(bf16)
            active_s[part * piece : (part + 1) * piece, units] = active
            slope = half + 2.0 * raised * half * (1.0 - half) * (
                0.7978845608028654 + 3.0 * 0.7978845608028654 * 0.044715 * square
            )
            raised_bar = (gate * bar_s[part, :, units].astype(f32) * slope).astype(bf16)
            bar_s[part, :, units] = raised_bar
            rows_bar = rows_bar + product_right(raised_bar, w_up_s[:, units])
            produced = produced + product(active, w_down_s[units, :])
            return produced, rows_bar

        zeros = jnp.zeros((piece, width), f32)
        produced, rows_bar = lax.fori_loop(0, tiles, through, (zeros, zeros))
        rows_bar_s[blocks] = rows_bar.astype(bf16).reshape(length, capacity, width)
        net.start_back(rows_bar_s, back_ref, back_send, back_receive, part)
        produced = produced.astype(bf16)
        produced_s[blocks] = produced.reshape(length, capacity, width)
        gate_bar = jnp.sum(upstream * produced.astype(f32), axis=1, keepdims=True)
        slot = lax.broadcasted_iota(jnp.int32, (length, capacity, 128), 1)
        lane = lax.broadcasted_iota(jnp.int32, (length, capacity, 128), 2)
        spread = jnp.broadcast_to(gate_bar, (piece, 128)).reshape(length, capacity, 128)
        line = jnp.sum(jnp.where(slot == lane, spread, 0.0), axis=1, keepdims=True)
        gate_s[blocks] = jnp.broadcast_to(line, (length, 8, 128))
        net.start_back(gate_s, gate_back_ref, gate_send, gate_receive, part)
    own_back = pltpu.make_async_copy(rows_bar_s.at[net.place], back_ref.at[net.me], local_sems.at[0])
    own_back.start()
    own_gate = pltpu.make_async_copy(gate_s.at[net.place], gate_back_ref.at[net.me], local_sems.at[1])
    own_gate.start()
    made = pltpu.make_async_copy(produced_s, produced_ref, local_sems.at[2])
    made.start()
    total = count * capacity
    rows_t_s[...] = rows_s[...].reshape(total, width).T
    copies = [None, None]
    for span in range(2 * tiles):
        side = span % 2
        units = pl.ds((span // 2) * tile, tile)
        if copies[side] is not None:
            copies[side].wait()
        if side == 0:
            bar = bar_s[:, :, units].reshape(total, tile)
            stage_s[side] = product(rows_t_s[...], bar).astype(bf16)
            goal = up_grad_ref.at[:, units]
        else:
            active_t = active_s[:, units].T
            stage_s[side] = product(active_t, scaled_s[...]).astype(bf16)
            goal = down_grad_ref.at[units, :]
        copies[side] = pltpu.make_async_copy(stage_s.at[side], goal, local_sems.at[4 + side])
        copies[side].start()
    for copy in copies:
        copy.wait()
    own_back.wait()
    own_gate.wait()
    made.wait()
    for part in range(net.parts):
        net.wait_out(sent_ref, rows_s, send, receive, part)
        net.wait_back(rows_bar_s, back_ref, back_send, back_receive, part)
        net.wait_back(gate_s, gate_back_ref, gate_send, gate_receive, part)
    net.wait_returns(back_ref, back_send, back_receive)
    net.wait_returns(gate_back_ref, gate_send, gate_receive)


def run_experts(n_wide, n_narrow, sent, upstream, w_up, w_down, w_router):
    count, capacity, width = sent.shape
    units = w_up.shape[1]
    total = count * capacity
    parts = min(4, n_wide)
    tile = min(768, units)
    dma = pltpu.SemaphoreType.DMA
    any_space = pl.BlockSpec(memory_space=pl.ANY)
    shape = jax.ShapeDtypeStruct
    return pl.pallas_call(
        functools.partial(experts_kernel, n_wide, n_narrow),
        out_shape=[
            shape((count, capacity, width), bf16),
            shape((count, 8, 128), f32),
            shape((count, capacity, width), bf16),
            shape((width, units), bf16),
            shape((units, width), bf16),
        ],
        in_specs=[any_space] * 4 + [pl.BlockSpec(memory_space=pltpu.VMEM)],
        out_specs=[any_space] * 5,
        scratch_shapes=[
            pltpu.VMEM((count, capacity, width), bf16),
            pltpu.VMEM((count, capacity, width), bf16),
            pltpu.VMEM((width, units), bf16),
            pltpu.VMEM((units, width), bf16),
            pltpu.VMEM((total, units), bf16),
            pltpu.VMEM((parts, total // parts, units), bf16),
            pltpu.VMEM((count, capacity, width), bf16),
            pltpu.VMEM((count, capacity, width), bf16),
            pltpu.VMEM((count, 8, 128), f32),
            pltpu.VMEM((total, width), bf16),
            pltpu.VMEM((width, total), bf16),
            pltpu.VMEM((2, tile, max(tile, width)), bf16),
            dma((count,)),
            dma((count,)),
            dma((count,)),
            dma((count,)),
            dma((count,)),
            dma((count,)),
            dma((6,)),
        ],
        compiler_params=pltpu.CompilerParams(collective_id=1, has_side_effects=True, vmem_limit_bytes=VMEM_LIMIT),
        cost_estimate=pl.CostEstimate(flops=36 * 10**9, bytes_accessed=40 * 10**6, transcendentals=4 * 10**6),
        name="experts",
    )(sent, upstream, w_up, w_down, w_router)


def local(
    tokens,
    gain_one,
    w_query,
    w_key,
    w_value,
    w_out,
    table,
    gain_two,
    w_router,
    w_up,
    w_down,
    routes,
    cotangent,
):
    count, width = tokens.shape
    experts = w_router.shape[1]
    n_wide, n_narrow = lax.axis_size("wide"), lax.axis_size("narrow")
    me = lax.axis_index("wide") * n_narrow + lax.axis_index("narrow")
    capacity = max(2, (5 * count + 4 * experts - 1) // (4 * experts))
    total = experts * capacity
    sequences = count // SEQ_LEN
    groups = HEADS // GROUP
    params = pltpu.CompilerParams(vmem_limit_bytes=VMEM_LIMIT)
    buckets = jnp.asarray(lane_buckets())
    shape = jax.ShapeDtypeStruct

    target_column, target_row, sent_upstream = pl.pallas_call(
        functools.partial(slots_kernel, capacity),
        out_shape=[shape((count, 1), jnp.int32), shape((1, count), jnp.int32), shape((total, width), bf16)],
        compiler_params=params,
        name="slots",
    )(routes, routes.reshape(1, count), cotangent)

    def exchange(rows):
        return lax.all_to_all(rows.reshape(experts, capacity, width), BOTH, 0, 0, tiled=True).reshape(total, width)

    net = Exchange(n_wide, n_narrow)
    order = jnp.concatenate(
        [
            jnp.stack([net.partner(part, place)[0] * n_narrow + net.partner(part, place)[1] for place in range(net.length)])
            for part in range(net.parts)
        ]
    )
    upstream_rows = exchange(sent_upstream).reshape(experts, capacity, width)[order]

    columns = pl.BlockSpec((count, COLUMNS), lambda g: (0, g))
    rows_t = pl.BlockSpec((COLUMNS, count), lambda g: (g, 0))
    weight = pl.BlockSpec((width, COLUMNS), lambda g: (0, g))
    weights_block = pl.BlockSpec((GROUP, sequences, SEQ_LEN, SEQ_LEN), lambda g: (g, 0, 0, 0))
    (
        hidden,
        normed_one,
        normed_t,
        query,
        key_t,
        value,
        weights,
        mixed_t,
        normed_two,
        probs,
        gate,
        sent_rows,
    ) = pl.pallas_call(
        functools.partial(forward_kernel, capacity),
        grid=(groups,),
        in_specs=[
            whole((count, width)),
            whole((1, width)),
            weight,
            weight,
            weight,
            pl.BlockSpec((COLUMNS, width), lambda g: (g, 0)),
            whole((BUCKETS, HEADS)),
            whole((SPAN, BUCKETS)),
            pl.BlockSpec(memory_space=pltpu.SMEM),
            whole((1, width)),
            whole((width, experts)),
            whole((count, 1)),
            whole((1, count)),
        ],
        out_specs=[
            whole((count, width)),
            whole((count, width)),
            whole((width, count)),
            columns,
            rows_t,
            columns,
            weights_block,
            rows_t,
            whole((count, width)),
            whole((count, experts)),
            whole((count, 1)),
            whole((total, width)),
        ],
        out_shape=[
            shape((count, width), f32),
            shape((count, width), bf16),
            shape((width, count), bf16),
            shape((count, width), bf16),
            shape((width, count), bf16),
            shape((count, width), bf16),
            shape((HEADS, sequences, SEQ_LEN, SEQ_LEN), bf16),
            shape((width, count), bf16),
            shape((count, width), bf16),
            shape((count, experts), f32),
            shape((count, 1), f32),
            shape((total, width), bf16),
        ],
        scratch_shapes=[
            pltpu.VMEM((HEADS, TILE, SPAN), f32),
            pltpu.VMEM((count, COLUMNS), bf16),
            pltpu.VMEM((COLUMNS, count), bf16),
            pltpu.VMEM((COLUMNS, count), bf16),
        ],
        compiler_params=params,
        cost_estimate=pl.CostEstimate(flops=14 * 10**9, bytes_accessed=40 * 10**6, transcendentals=10**7),
        name="attention_forward",
    )(
        tokens,
        gain_one[None],
        w_query,
        w_key,
        w_value,
        w_out,
        table,
        buckets,
        table,
        gain_two[None],
        w_router,
        routes,
        target_row,
    )

    returned_bar, gate_lines, produced, up_grad, down_grad = run_experts(
        n_wide,
        n_narrow,
        sent_rows.reshape(experts, capacity, width),
        upstream_rows.reshape(experts, capacity, width),
        w_up[0],
        w_down[0],
        w_router,
    )
    def once(block):
        return pl.BlockSpec(block, lambda g: (0,) * len(block), pipeline_mode=pl.Buffered(1))

    any_space = pl.BlockSpec(memory_space=pl.ANY)
    vmem_space = pl.BlockSpec(memory_space=pltpu.VMEM)
    bits = len(bits_of(n_wide, n_narrow))
    parts = groups + 2
    *_, small_height = small_rows(experts)
    large = (width, width)
    small_shape = (small_height, width)
    part_shapes = [(large, bf16)] * (groups + 1) + [(small_shape, f32)]
    scratch = [pltpu.VMEM(*part) for part in part_shapes] * 2
    for part, (form, kind) in enumerate(part_shapes):
        scratch += received_shapes(form, kind, bits, min(bits, 4 if part == parts - 1 else 5), True)
    steps = 2 * bits
    dma = pltpu.SemaphoreType.DMA
    returned, tokens_grad, *reduced = pl.pallas_call(
        functools.partial(backward_kernel, n_wide, n_narrow, groups),
        grid=(groups,),
        in_specs=[
            any_space,
            once((total, width)),
            once((experts, 128)),
            once((count, 1)),
            once((count, 1)),
            any_space,
            any_space,
            once((count, experts)),
            once((count, 1)),
            once((1, width)),
            once((width, experts)),
            once((width, count)),
            once((width, width)),
            any_space,
            once((1, width)),
            columns,
            rows_t,
            columns,
            weights_block,
            once((width, count)),
            weight,
            weight,
            weight,
            once((SPAN, BUCKETS)),
        ],
        out_specs=[any_space] * (2 + parts),
        out_shape=[shape((experts, capacity, width), bf16), shape((count, width), bf16)]
        + [shape(form, kind) for form, kind in part_shapes],
        scratch_shapes=scratch
        + [
            pltpu.VMEM((count, width), f32),
            pltpu.VMEM((count, width), bf16),
            pltpu.VMEM((count, width), bf16),
            pltpu.VMEM((width, count), bf16),
            pltpu.VMEM((count, width), f32),
            pltpu.VMEM((SEQ_LEN, SEQ_LEN), bf16),
            pltpu.VMEM((COLUMNS, count), bf16),
            pltpu.VMEM((count, COLUMNS), bf16),
            pltpu.VMEM((count, COLUMNS), bf16),
            pltpu.VMEM((count, COLUMNS), bf16),
            pltpu.VMEM((TILE, SPAN), f32),
            pltpu.VMEM((2, 8, TILE), f32),
            pltpu.VMEM((16, SPAN), f32),
            dma((parts, steps)),
            dma((parts, steps)),
            dma((experts,)),
            dma((experts,)),
            dma((5 + parts,)),
        ],
        compiler_params=pltpu.CompilerParams(collective_id=0, has_side_effects=True, vmem_limit_bytes=61 * 2**20),
        cost_estimate=pl.CostEstimate(flops=24 * 10**9, bytes_accessed=40 * 10**6, transcendentals=0),
        name="attention_backward",
    )(
        produced,
        returned_bar.reshape(total, width),
        gate_lines[:, 0, :],
        target_column,
        routes,
        hidden,
        cotangent,
        probs,
        gate,
        gain_two[None],
        w_router,
        mixed_t,
        w_out,
        tokens,
        gain_one[None],
        query,
        key_t,
        value,
        weights,
        normed_t,
        w_query,
        w_key,
        w_value,
        buckets,
    )
    placing = (target_column == jnp.arange(total, dtype=jnp.int32)[None, :]).astype(bf16)
    gathered = product(placing, returned.reshape(total, width))
    output = (hidden + gate * gathered).astype(bf16)
    packed = reduced[-1]
    router_end, gain_two_at, gain_one_at, _ = small_rows(experts)
    router_grad = packed[:router_end].T
    gain_two_grad = packed[gain_two_at]
    gain_one_grad = packed[gain_one_at]
    table_grad = packed[router_end : router_end + HEADS, :BUCKETS].T

    def joined(index):
        return jnp.concatenate(
            [part[:, index * COLUMNS : (index + 1) * COLUMNS] for part in reduced[1:-1]], axis=1
        ).astype(f32)

    return (
        output,
        tokens_grad,
        gain_one_grad,
        joined(0),
        joined(1),
        joined(2),
        reduced[0].astype(f32),
        table_grad,
        gain_two_grad,
        router_grad,
        up_grad.astype(f32)[None],
        down_grad.astype(f32)[None],
    )


def solution(mesh):
    split = P(BOTH, None)
    experts = P(BOTH, None, None)
    in_specs = (split, P(), P(), P(), P(), P(), P(), P(), P(), experts, experts, split, split)
    out_specs = (split, split, P(), P(), P(), P(), P(), P(), P(), P(), experts, experts)
    return jax.shard_map(local, mesh=mesh, in_specs=in_specs, out_specs=out_specs, check_vma=False)
```

```python
import functools

import jax
import jax.numpy as jnp
import numpy as np
from jax import lax
from jax.experimental import pallas as pl
from jax.experimental.pallas import tpu as pltpu
from jax.sharding import PartitionSpec as P

HEADS = 12
HEAD_DIM = 64
BUCKETS = 32
SEQ_LEN = 512
EPSILON = 1e-06
LIMITS = (12, 16, 23, 32, 46, 64, 91)
HIGHEST = lax.Precision.HIGHEST
MESH = pl.DeviceIdType.MESH
BOTH = ("wide", "narrow")
GROUP = 4
COLUMNS = GROUP * HEAD_DIM
TILE = 128
SPAN = 512
HALF = 256
PIECE = 256
VMEM_LIMIT = 56 * 2**20

bf16 = jnp.bfloat16
f32 = jnp.float32


def product(left, right, **options):
    return jnp.dot(left, right, preferred_element_type=f32, **options)


def product_left(left, right, **options):
    return lax.dot_general(left, right, (((0,), (0,)), ((), ())), preferred_element_type=f32, **options)


def product_right(left, right, **options):
    return lax.dot_general(left, right, (((1,), (1,)), ((), ())), preferred_element_type=f32, **options)


def gelu_curve(values):
    return jax.nn.gelu(values, approximate=True)


def lane_buckets():
    offset = SPAN // 2 - np.arange(SPAN)
    distance = np.abs(offset)
    further = 8 + sum((distance >= limit).astype(np.int32) for limit in LIMITS)
    bucket = np.where(distance < 8, distance, further) + 16 * (offset > 0)
    return (bucket[:, None] == np.arange(BUCKETS)[None, :]).astype(np.float32)


def whole(shape):
    return pl.BlockSpec(shape, lambda *_: (0,) * len(shape))


def find_slots(capacity, experts, row_ref, target_row_ref):
    count = row_ref.shape[1]
    token_down = lax.broadcasted_iota(jnp.int32, (count, count), 0)
    token_across = lax.broadcasted_iota(jnp.int32, (count, count), 1)
    row = row_ref[...]
    picks = row == lax.broadcasted_iota(jnp.int32, (experts, count), 0)
    before = product(picks.astype(bf16), (token_down < token_across).astype(bf16))
    slot = jnp.sum(jnp.where(picks, before, 0.0), axis=0, keepdims=True).astype(jnp.int32)
    target_row_ref[...] = jnp.where(slot < capacity, row * capacity + slot, -1)


def as_column(row):
    return jnp.broadcast_to(row, (8, row.shape[1])).T[:, 0:1]


def place_part(net, part, target_row_ref, rows_ref, sent_ref):
    capacity, width = sent_ref.shape[1:]
    first = net.partner(part, 0)[0] // net.rows * net.length
    size = net.length * capacity
    slots = first * capacity + lax.broadcasted_iota(jnp.int32, (size, rows_ref.shape[0]), 0)
    placing = (slots == target_row_ref[...]).astype(bf16)
    rows = product(placing, rows_ref[...]).astype(bf16)
    sent_ref[pl.ds(first, net.length)] = rows.reshape(net.length, capacity, width)


def forward_kernel(
    n_wide,
    n_narrow,
    groups,
    cotangent_ref,
    tokens_ref,
    gain_one_ref,
    w_query_ref,
    w_key_ref,
    w_value_ref,
    w_out_ref,
    table_ref,
    buckets_ref,
    gain_two_ref,
    row_ref,
    hidden_ref,
    normed_ref,
    normed_t_ref,
    query_ref,
    key_t_ref,
    value_ref,
    weights_ref,
    mixed_t_ref,
    normed_two_ref,
    target_column_ref,
    target_row_ref,
    upstream_ref,
    curves,
    far_s,
    key_rows,
    query_t,
    value_t,
    sent_s,
    send,
    receive,
    own_sem,
):
    group = pl.program_id(0)
    count, width = tokens_ref.shape
    experts, capacity = upstream_ref.shape[:2]
    sequences = count // SEQ_LEN
    net = Exchange(n_wide, n_narrow)
    own_copy = pltpu.make_async_copy(sent_s.at[net.me], upstream_ref.at[net.place], own_sem)

    @pl.when(group == 0)
    def _():
        net.announce()
        find_slots(capacity, experts, row_ref, target_row_ref)
        for turn, part in enumerate(ISSUE):
            if part < net.parts:
                place_part(net, part, target_row_ref, cotangent_ref, sent_s)
                if turn == 0:
                    net.greet()
                net.start_out(sent_s, upstream_ref, send, receive, part)
        own_copy.start()
        target_column_ref[...] = as_column(target_row_ref[...])
        inputs = tokens_ref[...].astype(f32)
        factor = lax.rsqrt(jnp.mean(inputs * inputs, axis=1, keepdims=True) + EPSILON)
        normed = (inputs * factor * gain_one_ref[...]).astype(bf16)
        normed_ref[...] = normed
        normed_t_ref[...] = normed.T
        hidden_ref[...] = inputs
        curve = lax.dot_general(
            table_ref[...], buckets_ref[...], (((1,), (1,)), ((), ())), preferred_element_type=f32, precision=HIGHEST
        )
        for head in range(HEADS):
            wide = jnp.broadcast_to(curve[head : head + 1, :], (TILE, SPAN))
            curves[head] = pltpu.roll(wide, 0, 1, stride=1, stride_axis=0)
            far_s[head, 0:1, :] = jnp.broadcast_to(curve[head : head + 1, SPAN - 1 : SPAN], (1, TILE))
            far_s[head, 1:2, :] = jnp.broadcast_to(curve[head : head + 1, 0:1], (1, TILE))

    normed = normed_ref[...]
    query = product(normed, w_query_ref[...]).astype(bf16)
    query_ref[...] = query
    query_t[...] = (query * jnp.asarray(HEAD_DIM**-0.5, bf16)).T
    key = product(normed, w_key_ref[...]).astype(bf16)
    key_rows[...] = key
    key_t_ref[...] = key.T
    value = product(normed, w_value_ref[...]).astype(bf16)
    value_ref[...] = value
    value_t[...] = value.T

    lane = lax.broadcasted_iota(jnp.int32, (SEQ_LEN, TILE), 1)
    for head in range(GROUP):
        pair = head // 2 * TILE
        mine = (lane // HEAD_DIM) == head % 2
        index = group * GROUP + head
        far_left = far_s[index, 0:1, :]
        far_right = far_s[index, 1:2, :]
        for sequence in range(sequences):
            rows = pl.ds(sequence * SEQ_LEN, SEQ_LEN)
            keys = jnp.where(mine, key_rows[rows, pair : pair + TILE], jnp.zeros((), bf16))
            for half in range(SEQ_LEN // HALF):
                columns = pl.ds(sequence * SEQ_LEN + half * HALF, HALF)
                raw = product(keys, query_t[pair : pair + TILE, columns])
                parts = []
                for down in range(SEQ_LEN // TILE):
                    line = []
                    for across in range(HALF // TILE):
                        step = down - (half * (HALF // TILE) + across)
                        block = raw[down * TILE : (down + 1) * TILE, across * TILE : (across + 1) * TILE]
                        if abs(step) <= 1:
                            begin = SPAN // 2 - step * TILE
                            bias = curves[index, :, begin : begin + TILE]
                        else:
                            bias = far_right if step > 0 else far_left
                        line.append(block + bias)
                    parts.append(jnp.concatenate(line, axis=1))
                scores = jnp.concatenate(parts, axis=0)
                maximum = jnp.max(scores, axis=0, keepdims=True)
                exponent = jnp.exp(scores - maximum)
                total = jnp.sum(exponent, axis=0, keepdims=True)
                weights = (exponent * (1.0 / total)).astype(bf16)
                weights_ref[head, sequence, :, half * HALF : (half + 1) * HALF] = weights
                mixed_t_ref[head * HEAD_DIM : (head + 1) * HEAD_DIM, columns] = product(
                    value_t[head * HEAD_DIM : (head + 1) * HEAD_DIM, rows], weights
                ).astype(bf16)
    hidden_ref[...] += product(mixed_t_ref[...].T, w_out_ref[...])

    @pl.when(group == pl.num_programs(0) - 1)
    def _():
        hidden = hidden_ref[...]
        factor = lax.rsqrt(jnp.mean(hidden * hidden, axis=1, keepdims=True) + EPSILON)
        normed_two_ref[...] = (hidden * factor * gain_two_ref[...]).astype(bf16)
        own_copy.wait()
        for part in range(net.parts):
            net.wait_out(sent_s, upstream_ref, send, receive, part)
            net.wait_arrivals(upstream_ref, send, receive, part)


def norm_back(values, gain, upstream):
    factor = lax.rsqrt(jnp.mean(values * values, axis=-1, keepdims=True) + EPSILON)
    plain = values * factor
    scaled = upstream * gain
    inner = jnp.mean(scaled * plain, axis=-1, keepdims=True)
    return factor * (scaled - plain * inner), jnp.sum(upstream * plain, axis=0, keepdims=True)


def small_rows(experts):
    return experts, experts + 16, experts + 17, -(-(experts + 18) // 64) * 64


def backward_kernel(
    n_wide,
    n_narrow,
    groups,
    produced_ref,
    returned_bar_ref,
    gate_lines_ref,
    target_ref,
    row_ref,
    hidden_ref,
    cotangent_ref,
    probs_ref,
    gate_ref,
    gain_two_ref,
    w_router_ref,
    mixed_t_ref,
    w_out_ref,
    tokens_ref,
    gain_one_ref,
    query_ref,
    key_t_ref,
    value_ref,
    weights_ref,
    normed_t_ref,
    w_query_ref,
    w_key_ref,
    w_value_ref,
    buckets_ref,
    *refs,
):
    plans = plans_of(n_wide, n_narrow, groups)
    parts = len(plans)
    returned_ref, result_ref, refs = refs[0], refs[1], refs[2:]
    outs, refs = refs[: THIRDS + 2], refs[THIRDS + 2 :]
    buffers, refs = refs[:parts], refs[parts:]
    sums, refs = refs[:parts], refs[parts:]
    works = []
    for part in range(parts):
        stages, lane_bit = plans[part]
        received, refs = refs[: len(stages)], refs[len(stages) :]
        works.append(Reduction(buffers[part], sums[part], received, refs[0], refs[1], stages, lane_bit))
        refs = refs[2:]
    (
        hidden_bar,
        tokens_grad_ref,
        mixed_bar,
        mixed_bar_t,
        normed_bar,
        scores_s,
        query_bar_t,
        query_rows,
        key_bar,
        value_bar,
        near,
        far,
        diagonals,
        chosen_s,
        back_send,
        back_receive,
        own_sems,
    ) = refs
    hidden_low = tokens_grad_ref
    group = pl.program_id(0)
    count, width = normed_bar.shape
    experts, capacity = produced_ref.shape[:2]
    total = experts * capacity
    sequences = count // SEQ_LEN
    scale = HEAD_DIM**-0.5
    net = Exchange(n_wide, n_narrow)
    router_end, gain_two_at, gain_one_at, _ = small_rows(experts)
    own_copy = pltpu.make_async_copy(produced_ref.at[net.place], returned_ref.at[net.me], own_sems.at[0])
    hidden_copy = pltpu.make_async_copy(hidden_ref, hidden_bar, own_sems.at[1])
    cotangent_copy = pltpu.make_async_copy(cotangent_ref, tokens_grad_ref, own_sems.at[2])
    tokens_copy = pltpu.make_async_copy(tokens_ref, mixed_bar, own_sems.at[3])
    small = buffers[-1]

    def give_back(turn):
        if turn < len(ISSUE) and ISSUE[turn] < net.parts:
            net.start_back(produced_ref, returned_ref, back_send, back_receive, ISSUE[turn])


    @pl.when(group == 0)
    def _():
        net.announce()
        hidden_copy.start()
        cotangent_copy.start()
        net.greet()
        give_back(0)
        own_copy.start()
        diagonals[...] = jnp.zeros_like(diagonals)
        small[...] = jnp.zeros_like(small)
        hidden_copy.wait()
        cotangent_copy.wait()

        chosen_s[...] = as_column(row_ref[...])

        def prologue(index, carry):
            rows = pl.ds(pl.multiple_of(index * PIECE, PIECE), PIECE)
            target = target_ref[rows, :]
            chosen = chosen_s[rows, :]
            placing = (target == lax.broadcasted_iota(jnp.int32, (PIECE, total), 1)).astype(bf16)
            normed_two_bar = product(placing, returned_bar_ref[...])
            picks = chosen == lax.broadcasted_iota(jnp.int32, (PIECE, experts), 1)
            lines = product(picks.astype(f32), gate_lines_ref[...], precision=HIGHEST)
            slots = (target - chosen * capacity) == lax.broadcasted_iota(jnp.int32, (PIECE, 128), 1)
            gate_bar = jnp.sum(jnp.where(slots, lines, 0.0), axis=1, keepdims=True)
            inner = gate_ref[rows, :] * gate_bar
            logits_bar = (probs_ref[rows, :] * (jnp.where(picks, gate_bar, 0.0) - inner)).astype(bf16)
            normed_two_bar = normed_two_bar + product(logits_bar, w_router_ref[...])
            hidden = hidden_bar[rows, :]
            factor = lax.rsqrt(jnp.mean(hidden * hidden, axis=1, keepdims=True) + EPSILON)
            normed_two = (hidden * factor * gain_two_ref[...]).astype(bf16)
            small[0:router_end, :] += product_left(logits_bar, normed_two)
            back, gain_part = norm_back(hidden, gain_two_ref[...], normed_two_bar)
            small[gain_two_at : gain_two_at + 1, :] += gain_part
            bar = tokens_grad_ref[rows, :].astype(f32) + back
            hidden_bar[rows, :] = bar
            low = bar.astype(bf16)
            hidden_low[rows, :] = low
            mixed_bar[rows, :] = product_right(low, w_out_ref[...]).astype(bf16)
            return carry

        lax.fori_loop(0, count // PIECE, prologue, 0)
        for third in range(THIRDS):
            columns = pl.ds(third * COLUMNS, COLUMNS)
            buffers[third][...] = product(mixed_t_ref[...], hidden_low[:, columns]).astype(bf16)
            works[third].start(0)
        mixed_bar_t[...] = product_right(w_out_ref[...], hidden_low[...]).astype(bf16)

    def tick(head):
        for now in range(groups):
            turn = now * GROUP + head
            active = [(part, turns.index(turn)) for part, turns in enumerate(ADVANCE) if turn in turns]
            sends = [index + 1 for index, at in enumerate(GIVE) if at == turn]

            @pl.when(group == now)
            def _(active=active, sends=sends):
                for index in sends:
                    give_back(index)
                for job, step in active:
                    for part in range(job * THIRDS, (job + 1) * THIRDS):
                        works[part].finish(step)
                        works[part].start(step + 1)

    lane = lax.broadcasted_iota(jnp.int32, (SEQ_LEN, TILE), 1)
    features = pl.ds(pl.multiple_of(group * COLUMNS, COLUMNS), COLUMNS)
    for head in range(GROUP):
        pair = pl.ds(pl.multiple_of(group * COLUMNS + head // 2 * TILE, TILE), TILE)
        local_pair = pl.ds(head // 2 * TILE, TILE)
        mine = (lane // HEAD_DIM) == head % 2
        feature = pl.ds(head * HEAD_DIM, HEAD_DIM)
        near[...] = jnp.zeros_like(near)
        far[...] = jnp.zeros_like(far)
        for sequence in range(sequences):
            rows = pl.ds(sequence * SEQ_LEN, SEQ_LEN)
            values = jnp.where(mine, value_ref[rows, local_pair], jnp.zeros((), bf16))
            for half in range(SEQ_LEN // HALF):
                columns = pl.ds(sequence * SEQ_LEN + half * HALF, HALF)
                probs_bar = product(values, mixed_bar_t[pair, columns])
                probs = weights_ref[head, sequence, :, half * HALF : (half + 1) * HALF].astype(f32)
                shared = probs * probs_bar
                summed = jnp.sum(shared, axis=0, keepdims=True)
                scores_bar = shared - probs * summed
                scores_s[:, half * HALF : (half + 1) * HALF] = scores_bar.astype(bf16)
                for down in range(SEQ_LEN // TILE):
                    for across in range(HALF // TILE):
                        step = down - (half * (HALF // TILE) + across)
                        block = scores_bar[down * TILE : (down + 1) * TILE, across * TILE : (across + 1) * TILE]
                        if abs(step) <= 1:
                            begin = SPAN // 2 - step * TILE
                            near[:, begin : begin + TILE] += block
                        else:
                            side = 1 if step > 0 else 0
                            far[side] += jnp.sum(block.reshape(TILE // 8, 8, TILE), axis=0)
            weights = weights_ref[head, sequence]
            scores_low = scores_s[...]
            value_part = product(weights, mixed_bar[rows, pair]).astype(bf16)
            key_part = (product(scores_low, query_ref[rows, local_pair]) * scale).astype(bf16)
            if head % 2 == 0:
                value_bar[rows, local_pair] = value_part
                key_bar[rows, local_pair] = key_part
            else:
                value_bar[rows, local_pair] = jnp.where(mine, value_part, value_bar[rows, local_pair])
                key_bar[rows, local_pair] = jnp.where(mine, key_part, key_bar[rows, local_pair])
            query_bar_t[feature, rows] = (product(key_t_ref[feature, rows], scores_low) * scale).astype(bf16)
        folded = near[0:8, :]
        for step in range(1, TILE // 8):
            folded = folded + pltpu.roll(near[8 * step : 8 * step + 8, :], SPAN - 8 * step, 1)
        place = lax.broadcasted_iota(jnp.int32, (8, SPAN), 0)
        for bit in (4, 2, 1):
            folded = jnp.where((place & bit) > 0, pltpu.roll(folded, SPAN - bit, 1), folded)
        gathered = jnp.sum(folded, axis=0, keepdims=True)
        place = lax.broadcasted_iota(jnp.int32, (1, SPAN), 1)
        left = jnp.sum(far[0])
        right = jnp.sum(far[1])
        gathered = gathered + jnp.where(place == SPAN - 1, left, 0.0) + jnp.where(place == 0, right, 0.0)
        diagonals[pl.ds(group * GROUP + head, 1), :] = gathered
        tick(head)

    @pl.when(group == groups - 1)
    def _():
        tokens_copy.start()

    query_bar = query_bar_t[...].T
    normed_t = normed_t_ref[...]
    query_rows[...] = query_bar
    for now in range(groups):

        @pl.when(group == now)
        def _(now=now):
            for index, part in enumerate((query_rows, key_bar, value_bar)):
                place = (now + 1) * THIRDS + index
                buffers[place][...] = product(normed_t, part[...]).astype(bf16)
                works[place].start(0)


    def project(index, carry):
        rows = pl.ds(pl.multiple_of(index * PIECE, PIECE), PIECE)
        bar = (
            product_right(query_rows[rows, :], w_query_ref[...])
            + product_right(key_bar[rows, :], w_key_ref[...])
            + product_right(value_bar[rows, :], w_value_ref[...])
        )

        @pl.when(group == 0)
        def _():
            normed_bar[rows, :] = bar

        @pl.when(group > 0)
        def _():
            normed_bar[rows, :] += bar

        @pl.when(group == groups - 1)
        def _():
            back, gain_part = norm_back(mixed_bar[rows, :].astype(f32), gain_one_ref[...], normed_bar[rows, :])
            tokens_grad_ref[rows, :] = (hidden_bar[rows, :] + back).astype(bf16)
            small[gain_one_at : gain_one_at + 1, :] += gain_part

        return carry

    @pl.when(group == groups - 1)
    def _():
        tokens_copy.wait()

    lax.fori_loop(0, count // PIECE, project, 0)

    @pl.when(group == groups - 1)
    def _():
        small[router_end : router_end + 16, 0:BUCKETS] = product(
            diagonals[...], buckets_ref[...], precision=HIGHEST
        )
        works[-1].start(0)
        at = [len(turns) for turns in ADVANCE for _ in range(THIRDS)] + [0]
        while any(step < work.steps for step, work in zip(at, works)):
            for part, work in enumerate(works):
                work.finish(at[part])
                work.start(at[part] + 1)
                at[part] += 1
        outward = [pltpu.make_async_copy(tokens_grad_ref, result_ref, own_sems.at[4])]
        for part in range(parts):
            job, third = divmod(part, THIRDS)
            if part == parts - 1:
                goal = outs[-1]
            elif job == 0:
                goal = outs[THIRDS].at[:, pl.ds(third * COLUMNS, COLUMNS)]
            else:
                goal = outs[third].at[:, pl.ds((job - 1) * COLUMNS, COLUMNS)]
            outward.append(pltpu.make_async_copy(sums[part], goal, own_sems.at[5 + part]))
        for copy in outward:
            copy.start()
        for copy in outward:
            copy.wait()
        own_copy.wait()
        for part in range(net.parts):
            net.wait_back(produced_ref, returned_ref, back_send, back_receive, part)
        net.wait_returns(returned_ref, back_send, back_receive)


def plan_of(n_wide, n_narrow, halvings, turn, size):
    bits = [("narrow", 1 << b) for b in range(n_narrow.bit_length() - 1)]
    bits += [("wide", 1 << b) for b in range(n_wide.bit_length() - 1)]
    if turn and len(bits) > 2:
        bits[1], bits[2] = bits[2], bits[1]
    stages, done = [], 0
    while done < len(bits):
        halve = done < halvings
        many = min(size if done >= 3 else 1, (halvings if halve else len(bits)) - done)
        stages.append((tuple(bits[done : done + many]), halve))
        done += many
    return stages, bits[0]


THIRDS = 3


def plans_of(n_wide, n_narrow, groups):
    plans = []
    for job in range(groups + 1):
        for third in range(THIRDS):
            plans.append(plan_of(n_wide, n_narrow, 5, (third + job) % 2, LAST if job == groups else OTHERS))
    return plans + [plan_of(n_wide, n_narrow, 3, 0, 2)]


class Reduction:
    def __init__(self, buffer, gathered, received, send, receive, stages, lane_bit):
        self.buffer, self.gathered, self.received = buffer, gathered, received
        self.send, self.receive = send, receive
        self.stages, self.lane_bit = stages, lane_bit
        self.place = {"wide": lax.axis_index("wide"), "narrow": lax.axis_index("narrow")}
        rows, lanes = buffer.shape
        self.regions = [((0, rows), (0, lanes))]
        for bits, halve in stages:
            region = self.regions[-1]
            self.regions.append(self.piece(region, bits, 0) if halve else region)
        self.back = [index for index, (_, halve) in enumerate(stages) if halve][::-1]
        self.steps = len(stages) + len(self.back)
        self.first = [0]
        for step in range(self.steps):
            self.first.append(self.first[-1] + self.others(step) )

    def stage_of(self, step):
        return step if step < len(self.stages) else self.back[step - len(self.stages)]

    def others(self, step):
        return 2 ** len(self.stages[self.stage_of(step)][0]) - 1

    def own(self, bit):
        return (self.place[bit[0]] // bit[1]) % 2

    def piece(self, region, bits, change):
        (row, rows), (lane, lanes) = region
        for index, bit in enumerate(bits):
            own = self.own(bit)
            if (change >> index) & 1:
                own = 1 - own
            if bit == self.lane_bit:
                lanes = lanes // 2
                lane = lane + own * lanes
            else:
                rows = rows // 2
                row = row + own * rows
        return (row, rows), (lane, lanes)

    def target(self, bits, change):
        place = dict(self.place)
        for index, bit in enumerate(bits):
            if (change >> index) & 1:
                place[bit[0]] = place[bit[0]] + bit[1] - 2 * bit[1] * self.own(bit)
        return place["wide"], place["narrow"]

    def view(self, buffer, region):
        (row, rows), (lane, lanes) = region
        row = row if isinstance(row, int) else pl.multiple_of(row, 16 if self.buffer.dtype == bf16 else 8)
        lane = lane if isinstance(lane, int) else pl.multiple_of(lane, 128)
        return buffer.at[pl.ds(row, rows), pl.ds(lane, lanes)]

    def copy(self, step, change):
        stage = self.stage_of(step)
        bits, halve = self.stages[stage]
        if step < len(self.stages):
            region = self.piece(self.regions[stage], bits, change) if halve else self.regions[stage]
            source, sink = self.view(self.buffer, region), self.received[stage].at[change - 1]
        else:
            source = sink = self.view(self.gathered, self.regions[stage + 1])
        index = self.first[step] + change - 1
        return pltpu.make_async_remote_copy(
            src_ref=source,
            dst_ref=sink,
            send_sem=self.send.at[index],
            recv_sem=self.receive.at[index],
            device_id=self.target(bits, change),
            device_id_type=MESH,
        )

    def start(self, step):
        if 0 <= step < self.steps:
            for change in range(1, self.others(step) + 1):
                self.copy(step, change).start()

    def finish(self, step):
        if not 0 <= step < self.steps:
            return
        for change in range(1, self.others(step) + 1):
            self.copy(step, change).wait()
        if step < len(self.stages):
            region = self.regions[step + 1]
            mine = self.view(self.buffer, region)
            result = mine if step < len(self.stages) - 1 else self.view(self.gathered, region)
            total = mine[...].astype(f32)
            for change in range(self.others(step)):
                total = total + self.received[step][change].astype(f32)
            result[...] = total.astype(mine.dtype)


def reduction_scratch(shape, dtype, stages, lane_bit):
    rows, lanes = shape
    received, copies = [], 0
    for bits, halve in stages:
        if halve:
            for bit in bits:
                if bit == lane_bit:
                    lanes //= 2
                else:
                    rows //= 2
        others = 2 ** len(bits) - 1
        received.append(pltpu.VMEM((others, rows, lanes), dtype))
        copies += others * (2 if halve else 1)
    return received, copies


class Exchange:
    def __init__(self, n_wide, n_narrow):
        self.n_wide, self.n_narrow = n_wide, n_narrow
        self.count = n_wide * n_narrow
        self.parts = min(4, n_wide)
        self.rows = n_wide // self.parts
        self.length = self.rows * n_narrow
        w, k = lax.axis_index("wide"), lax.axis_index("narrow")
        self.me = w * n_narrow + k
        self.top, self.place = w // self.rows, (w % self.rows) * n_narrow + k

    def partner(self, part, place):
        top, bit = self.top, 1
        while bit < self.parts:
            if part & bit:
                top = top + bit - 2 * bit * ((top // bit) % 2)
            bit *= 2
        w = top * self.rows + place // self.n_narrow
        return w, place % self.n_narrow

    def each(self, part, act):
        def body(place, carry):
            if part == 0:

                @pl.when(place != self.place)
                def _():
                    act(place)

            else:
                act(place)
            return carry

        lax.fori_loop(0, self.length, body, 0)

    def announce(self):
        barrier = pltpu.get_barrier_semaphore()
        for part in range(self.parts):

            def act(place, part=part):
                pl.semaphore_signal(barrier, inc=1, device_id=self.partner(part, place), device_id_type=MESH)

            self.each(part, act)

    def greet(self):
        pl.semaphore_wait(pltpu.get_barrier_semaphore(), self.count - 1)

    def out(self, source, sink, send, receive, part, place):
        w, k = self.partner(part, place)
        slot = part * self.length
        return pltpu.make_async_remote_copy(
            src_ref=source.at[w * self.n_narrow + k],
            dst_ref=sink.at[slot + self.place],
            send_sem=send.at[slot + place],
            recv_sem=receive.at[slot + self.place],
            device_id=(w, k),
            device_id_type=MESH,
        )

    def back(self, source, sink, send, receive, part, place):
        slot = part * self.length + place
        return pltpu.make_async_remote_copy(
            src_ref=source.at[slot],
            dst_ref=sink.at[self.me],
            send_sem=send.at[slot],
            recv_sem=receive.at[self.me],
            device_id=self.partner(part, place),
            device_id_type=MESH,
        )

    def arrival(self, sink, send, receive, slot):
        return pltpu.make_async_remote_copy(
            src_ref=sink.at[slot],
            dst_ref=sink.at[slot],
            send_sem=send.at[slot],
            recv_sem=receive.at[slot],
            device_id=self.partner(self.parts - 1, self.place),
            device_id_type=MESH,
        )

    def start_out(self, source, sink, send, receive, part):
        self.each(part, lambda place: self.out(source, sink, send, receive, part, place).start())

    def wait_out(self, source, sink, send, receive, part):
        self.each(part, lambda place: self.out(source, sink, send, receive, part, place).wait_send())

    def wait_arrivals(self, sink, send, receive, part):
        slot = part * self.length
        self.each(part, lambda place: self.arrival(sink, send, receive, slot + place).wait_recv())

    def start_back(self, source, sink, send, receive, part):
        self.each(part, lambda place: self.back(source, sink, send, receive, part, place).start())

    def wait_back(self, source, sink, send, receive, part):
        self.each(part, lambda place: self.back(source, sink, send, receive, part, place).wait_send())

    def wait_returns(self, sink, send, receive):
        def body(slot, carry):
            @pl.when(slot != self.me)
            def _():
                self.arrival(sink, send, receive, slot).wait_recv()

            return carry

        lax.fori_loop(0, self.count, body, 0)


ISSUE = (2, 3, 1, 0)
ADVANCE = ((3, 7, 11), (7, 11), (11,), ())
OTHERS, LAST = 2, 2
GIVE = (3, 7, 11)


def experts_kernel(
    n_wide,
    n_narrow,
    target_row_ref,
    row_ref,
    normed_two_ref,
    w_router_ref,
    upstream_ref,
    w_up_ref,
    w_down_ref,
    probs_ref,
    gate_ref,
    back_ref,
    gate_back_ref,
    produced_ref,
    up_grad_ref,
    down_grad_ref,
    sent_ref,
    rows_s,
    upstream_s,
    w_up_s,
    w_down_s,
    active_s,
    bar_s,
    rows_bar_s,
    produced_s,
    gate_s,
    scaled_s,
    rows_t_s,
    stage_s,
    send,
    receive,
    back_send,
    back_receive,
    gate_send,
    gate_receive,
    local_sems,
):
    net = Exchange(n_wide, n_narrow)
    count, capacity, width = rows_s.shape
    length = net.length
    piece = length * capacity
    hidden_units = w_up_s.shape[1]
    tile = min(768, hidden_units)
    tiles = hidden_units // tile
    net.announce()
    down_copy = pltpu.make_async_copy(w_down_ref, w_down_s, local_sems.at[0])
    down_copy.start()
    upstream_copy = pltpu.make_async_copy(upstream_ref, upstream_s, local_sems.at[1])
    upstream_copy.start()
    up_copy = pltpu.make_async_copy(w_up_ref, w_up_s, local_sems.at[2])
    up_copy.start()
    own_copy = pltpu.make_async_copy(sent_ref.at[net.me], rows_s.at[net.place], local_sems.at[3])
    for turn, part in enumerate(ISSUE):
        if part < net.parts:
            place_part(net, part, target_row_ref, normed_two_ref, sent_ref)
            if turn == 0:
                net.greet()
            net.start_out(sent_ref, rows_s, send, receive, part)
    own_copy.start()
    down_copy.wait()
    upstream_copy.wait()

    def before(index, carry):
        part, span = index // tiles, index % tiles
        units = pl.ds(pl.multiple_of(span * tile, tile), tile)
        upstream = upstream_s[pl.ds(part * length, length)].reshape(piece, width)
        bar_s[part, :, units] = product_right(upstream, w_down_s[units, :]).astype(bf16)
        return carry

    lax.fori_loop(0, net.parts * tiles, before, 0)
    up_copy.wait()
    own_copy.wait()
    for part in (0, 2, 1, 3):
        net.wait_arrivals(rows_s, send, receive, part)
        blocks = pl.ds(part * length, length)
        rows = rows_s[blocks].reshape(piece, width)
        upstream = upstream_s[blocks].reshape(piece, width).astype(f32)
        logits = product_right(rows, w_router_ref[...])
        exponent = jnp.exp(logits - jnp.max(logits, axis=1, keepdims=True))
        probs = exponent / jnp.sum(exponent, axis=1, keepdims=True)
        mine = lax.broadcasted_iota(jnp.int32, probs.shape, 1) == net.me
        gate = jnp.sum(jnp.where(mine, probs, 0.0), axis=1, keepdims=True)
        scaled_s[part * piece : (part + 1) * piece, :] = (gate * upstream).astype(bf16)

        def through(span, carry):
            produced, rows_bar = carry
            units = pl.ds(pl.multiple_of(span * tile, tile), tile)
            raised = product(rows, w_up_s[:, units])
            square = raised * raised
            inner = raised * (0.7978845608028654 + 0.7978845608028654 * 0.044715 * square)
            half = 0.5 + 0.5 * jnp.tanh(inner)
            active = (raised * half).astype(bf16)
            active_s[part * piece : (part + 1) * piece, units] = active
            slope = half + 2.0 * raised * half * (1.0 - half) * (
                0.7978845608028654 + 3.0 * 0.7978845608028654 * 0.044715 * square
            )
            raised_bar = (gate * bar_s[part, :, units].astype(f32) * slope).astype(bf16)
            bar_s[part, :, units] = raised_bar
            rows_bar = rows_bar + product_right(raised_bar, w_up_s[:, units])
            produced = produced + product(active, w_down_s[units, :])
            return produced, rows_bar

        zeros = jnp.zeros((piece, width), f32)
        produced, rows_bar = lax.fori_loop(0, tiles, through, (zeros, zeros))
        rows_bar_s[blocks] = rows_bar.astype(bf16).reshape(length, capacity, width)
        net.start_back(rows_bar_s, back_ref, back_send, back_receive, part)
        produced = produced.astype(bf16)
        produced_s[blocks] = produced.reshape(length, capacity, width)
        gate_bar = jnp.sum(upstream * produced.astype(f32), axis=1, keepdims=True)
        slot = lax.broadcasted_iota(jnp.int32, (length, capacity, 128), 1)
        lane = lax.broadcasted_iota(jnp.int32, (length, capacity, 128), 2)
        spread = jnp.broadcast_to(gate_bar, (piece, 128)).reshape(length, capacity, 128)
        line = jnp.sum(jnp.where(slot == lane, spread, 0.0), axis=1, keepdims=True)
        gate_s[blocks] = jnp.broadcast_to(line, (length, 8, 128))
        net.start_back(gate_s, gate_back_ref, gate_send, gate_receive, part)
    logits = product_right(normed_two_ref[...], w_router_ref[...])
    exponent = jnp.exp(logits - jnp.max(logits, axis=1, keepdims=True))
    probs = exponent / jnp.sum(exponent, axis=1, keepdims=True)
    probs_ref[...] = probs
    picks = as_column(row_ref[...]) == lax.broadcasted_iota(jnp.int32, probs.shape, 1)
    gate_ref[...] = jnp.sum(jnp.where(picks, probs, 0.0), axis=1, keepdims=True)
    own_back = pltpu.make_async_copy(rows_bar_s.at[net.place], back_ref.at[net.me], local_sems.at[0])
    own_back.start()
    own_gate = pltpu.make_async_copy(gate_s.at[net.place], gate_back_ref.at[net.me], local_sems.at[1])
    own_gate.start()
    made = pltpu.make_async_copy(produced_s, produced_ref, local_sems.at[2])
    made.start()
    total = count * capacity
    rows_t_s[...] = rows_s[...].reshape(total, width).T
    copies = [None, None]
    for span in range(2 * tiles):
        side = span % 2
        units = pl.ds((span // 2) * tile, tile)
        if copies[side] is not None:
            copies[side].wait()
        if side == 0:
            bar = bar_s[:, :, units].reshape(total, tile)
            stage_s[side] = product(rows_t_s[...], bar).astype(bf16)
            goal = up_grad_ref.at[:, units]
        else:
            active_t = active_s[:, units].T
            stage_s[side] = product(active_t, scaled_s[...]).astype(bf16)
            goal = down_grad_ref.at[units, :]
        copies[side] = pltpu.make_async_copy(stage_s.at[side], goal, local_sems.at[4 + side])
        copies[side].start()
    for copy in copies:
        copy.wait()
    own_back.wait()
    own_gate.wait()
    made.wait()
    for part in range(net.parts):
        net.wait_out(sent_ref, rows_s, send, receive, part)
        net.wait_back(rows_bar_s, back_ref, back_send, back_receive, part)
        net.wait_back(gate_s, gate_back_ref, gate_send, gate_receive, part)
    net.wait_returns(back_ref, back_send, back_receive)
    net.wait_returns(gate_back_ref, gate_send, gate_receive)


def run_experts(n_wide, n_narrow, target_row, routes, normed_two, w_router, upstream, w_up, w_down):
    count, capacity, width = upstream.shape
    tokens, experts = normed_two.shape[0], w_router.shape[0]
    units = w_up.shape[1]
    total = count * capacity
    parts = min(4, n_wide)
    tile = min(768, units)
    dma = pltpu.SemaphoreType.DMA
    any_space = pl.BlockSpec(memory_space=pl.ANY)
    shape = jax.ShapeDtypeStruct
    return pl.pallas_call(
        functools.partial(experts_kernel, n_wide, n_narrow),
        out_shape=[
            shape((tokens, experts), f32),
            shape((tokens, 1), f32),
            shape((count, capacity, width), bf16),
            shape((count, 8, 128), f32),
            shape((count, capacity, width), bf16),
            shape((width, units), bf16),
            shape((units, width), bf16),
        ],
        in_specs=[pl.BlockSpec(memory_space=pltpu.VMEM)] * 4 + [any_space] * 3,
        out_specs=[pl.BlockSpec(memory_space=pltpu.VMEM)] * 2 + [any_space] * 5,
        scratch_shapes=[
            pltpu.VMEM((count, capacity, width), bf16),
            pltpu.VMEM((count, capacity, width), bf16),
            pltpu.VMEM((count, capacity, width), bf16),
            pltpu.VMEM((width, units), bf16),
            pltpu.VMEM((units, width), bf16),
            pltpu.VMEM((total, units), bf16),
            pltpu.VMEM((parts, total // parts, units), bf16),
            pltpu.VMEM((count, capacity, width), bf16),
            pltpu.VMEM((count, capacity, width), bf16),
            pltpu.VMEM((count, 8, 128), f32),
            pltpu.VMEM((total, width), bf16),
            pltpu.VMEM((width, total), bf16),
            pltpu.VMEM((2, tile, max(tile, width)), bf16),
            dma((count,)),
            dma((count,)),
            dma((count,)),
            dma((count,)),
            dma((count,)),
            dma((count,)),
            dma((6,)),
        ],
        compiler_params=pltpu.CompilerParams(collective_id=1, has_side_effects=True, vmem_limit_bytes=VMEM_LIMIT),
        cost_estimate=pl.CostEstimate(flops=36 * 10**9, bytes_accessed=40 * 10**6, transcendentals=4 * 10**6),
        name="experts",
    )(target_row, routes, normed_two, w_router, upstream, w_up, w_down)


def finish_kernel(
    returned_ref,
    target_ref,
    gate_ref,
    hidden_ref,
    up_ref,
    down_ref,
    query_ref,
    key_ref,
    value_ref,
    out_ref,
    small_ref,
    output_ref,
    up_grad_ref,
    down_grad_ref,
    query_grad_ref,
    key_grad_ref,
    value_grad_ref,
    out_grad_ref,
    router_grad_ref,
    table_grad_ref,
    gain_one_grad_ref,
    gain_two_grad_ref,
):
    total = returned_ref.shape[0]
    placing = (target_ref[...] == lax.broadcasted_iota(jnp.int32, (target_ref.shape[0], total), 1)).astype(bf16)
    gathered = product(placing, returned_ref[...])
    output_ref[...] = (hidden_ref[...] + gate_ref[...] * gathered).astype(bf16)
    up_grad_ref[...] = up_ref[...].astype(f32)
    down_grad_ref[...] = down_ref[...].astype(f32)
    query_grad_ref[...] = query_ref[...].astype(f32)
    key_grad_ref[...] = key_ref[...].astype(f32)
    value_grad_ref[...] = value_ref[...].astype(f32)
    out_grad_ref[...] = out_ref[...].astype(f32)

    @pl.when(pl.program_id(0) == 0)
    def _():
        experts = router_grad_ref.shape[0]
        router_end, gain_two_at, gain_one_at, _ = small_rows(experts)
        router_grad_ref[...] = small_ref[0:router_end, :]
        table_grad_ref[...] = small_ref[router_end : router_end + HEADS, 0:BUCKETS]
        gain_one_grad_ref[...] = small_ref[gain_one_at : gain_one_at + 1, :]
        gain_two_grad_ref[...] = small_ref[gain_two_at : gain_two_at + 1, :]


def local(
    tokens,
    gain_one,
    w_query,
    w_key,
    w_value,
    w_out,
    table,
    gain_two,
    w_router,
    w_up,
    w_down,
    routes,
    cotangent,
):
    count, width = tokens.shape
    experts = w_router.shape[1]
    n_wide, n_narrow = lax.axis_size("wide"), lax.axis_size("narrow")
    me = lax.axis_index("wide") * n_narrow + lax.axis_index("narrow")
    capacity = max(2, (5 * count + 4 * experts - 1) // (4 * experts))
    total = experts * capacity
    sequences = count // SEQ_LEN
    groups = HEADS // GROUP
    params = pltpu.CompilerParams(vmem_limit_bytes=VMEM_LIMIT)
    gain_one, gain_two = gain_one.reshape(1, width), gain_two.reshape(1, width)
    routes, w_router = routes.reshape(1, count), w_router.T
    buckets = jnp.asarray(lane_buckets())
    shape = jax.ShapeDtypeStruct

    any_space = pl.BlockSpec(memory_space=pl.ANY)
    dma = pltpu.SemaphoreType.DMA
    columns = pl.BlockSpec((count, COLUMNS), lambda g: (0, g))
    rows_t = pl.BlockSpec((COLUMNS, count), lambda g: (g, 0))
    weight = pl.BlockSpec((width, COLUMNS), lambda g: (0, g))
    weights_block = pl.BlockSpec((GROUP, sequences, SEQ_LEN, SEQ_LEN), lambda g: (g, 0, 0, 0))
    (
        hidden,
        normed_one,
        normed_t,
        query,
        key_t,
        value,
        weights,
        mixed_t,
        normed_two,
        target_column,
        target_row,
        upstream_rows,
    ) = pl.pallas_call(
        functools.partial(forward_kernel, n_wide, n_narrow, groups),
        grid=(groups,),
        in_specs=[
            whole((count, width)),
            whole((count, width)),
            whole((1, width)),
            weight,
            weight,
            weight,
            pl.BlockSpec((COLUMNS, width), lambda g: (g, 0)),
            whole((HEADS, BUCKETS)),
            whole((SPAN, BUCKETS)),
            whole((1, width)),
            whole((1, count)),
        ],
        out_specs=[
            whole((count, width)),
            whole((count, width)),
            whole((width, count)),
            columns,
            rows_t,
            columns,
            weights_block,
            rows_t,
            whole((count, width)),
            whole((count, 1)),
            whole((1, count)),
            any_space,
        ],
        out_shape=[
            shape((count, width), f32),
            shape((count, width), bf16),
            shape((width, count), bf16),
            shape((count, width), bf16),
            shape((width, count), bf16),
            shape((count, width), bf16),
            shape((HEADS, sequences, SEQ_LEN, SEQ_LEN), bf16),
            shape((width, count), bf16),
            shape((count, width), bf16),
            shape((count, 1), jnp.int32),
            shape((1, count), jnp.int32),
            shape((experts, capacity, width), bf16),
        ],
        scratch_shapes=[
            pltpu.VMEM((HEADS, TILE, SPAN), f32),
            pltpu.VMEM((HEADS, 8, TILE), f32),
            pltpu.VMEM((count, COLUMNS), bf16),
            pltpu.VMEM((COLUMNS, count), bf16),
            pltpu.VMEM((COLUMNS, count), bf16),
            pltpu.VMEM((experts, capacity, width), bf16),
            dma((experts,)),
            dma((experts,)),
            dma,
        ],
        compiler_params=pltpu.CompilerParams(collective_id=2, has_side_effects=True, vmem_limit_bytes=VMEM_LIMIT),
        cost_estimate=pl.CostEstimate(flops=14 * 10**9, bytes_accessed=40 * 10**6, transcendentals=10**7),
        name="attention_forward",
    )(
        cotangent,
        tokens,
        gain_one,
        w_query,
        w_key,
        w_value,
        w_out,
        table.T,
        buckets,
        gain_two,
        routes,
    )

    probs, gate, returned_bar, gate_lines, produced, up_grad, down_grad = run_experts(
        n_wide, n_narrow, target_row, routes, normed_two, w_router, upstream_rows, w_up[0], w_down[0]
    )

    def once(block):
        return pl.BlockSpec(block, lambda g: (0,) * len(block), pipeline_mode=pl.Buffered(1))

    plans = plans_of(n_wide, n_narrow, groups)
    *_, small_height = small_rows(experts)
    third = (width, COLUMNS)
    small_shape = (small_height, width)
    part_shapes = [(third, bf16)] * (len(plans) - 1) + [(small_shape, f32)]
    parts = len(part_shapes)
    scratch = [pltpu.VMEM(*part) for part in part_shapes] * 2
    for part, (form, kind) in enumerate(part_shapes):
        received, copies = reduction_scratch(form, kind, *plans[part])
        scratch += received + [pltpu.SemaphoreType.DMA((copies,))] * 2
    returned, tokens_grad, query_grad, key_grad, value_grad, out_grad, small = pl.pallas_call(
        functools.partial(backward_kernel, n_wide, n_narrow, groups),
        grid=(groups,),
        in_specs=[
            any_space,
            once((total, width)),
            once((experts, 128)),
            once((count, 1)),
            once((1, count)),
            any_space,
            any_space,
            once((count, experts)),
            once((count, 1)),
            once((1, width)),
            once((experts, width)),
            once((width, count)),
            once((width, width)),
            any_space,
            once((1, width)),
            columns,
            rows_t,
            columns,
            weights_block,
            once((width, count)),
            weight,
            weight,
            weight,
            once((SPAN, BUCKETS)),
        ],
        out_specs=[any_space] * (THIRDS + 4),
        out_shape=[shape((experts, capacity, width), bf16), shape((count, width), bf16)]
        + [shape((width, width), bf16)] * (THIRDS + 1)
        + [shape(small_shape, f32)],
        scratch_shapes=scratch
        + [
            pltpu.VMEM((count, width), f32),
            pltpu.VMEM((count, width), bf16),
            pltpu.VMEM((count, width), bf16),
            pltpu.VMEM((width, count), bf16),
            pltpu.VMEM((count, width), f32),
            pltpu.VMEM((SEQ_LEN, SEQ_LEN), bf16),
            pltpu.VMEM((COLUMNS, count), bf16),
            pltpu.VMEM((count, COLUMNS), bf16),
            pltpu.VMEM((count, COLUMNS), bf16),
            pltpu.VMEM((count, COLUMNS), bf16),
            pltpu.VMEM((TILE, SPAN), f32),
            pltpu.VMEM((2, 8, TILE), f32),
            pltpu.VMEM((16, SPAN), f32),
            pltpu.VMEM((count, 1), jnp.int32),
            dma((experts,)),
            dma((experts,)),
            dma((5 + parts,)),
        ],
        compiler_params=pltpu.CompilerParams(collective_id=0, has_side_effects=True, vmem_limit_bytes=61 * 2**20),
        cost_estimate=pl.CostEstimate(flops=24 * 10**9, bytes_accessed=40 * 10**6, transcendentals=0),
        name="attention_backward",
    )(
        produced,
        returned_bar.reshape(total, width),
        gate_lines[:, 0, :],
        target_column,
        routes,
        hidden,
        cotangent,
        probs,
        gate,
        gain_two,
        w_router,
        mixed_t,
        w_out,
        tokens,
        gain_one,
        query,
        key_t,
        value,
        weights,
        normed_t,
        w_query,
        w_key,
        w_value,
        buckets,
    )
    steps = 8

    def slab(*form):
        return pl.BlockSpec((form[0] // steps,) + form[1:], lambda g: (g, 0))

    units = up_grad.shape[1]
    matrix = slab(width, width)
    output, up_grad, down_grad, query_grad, key_grad, value_grad, out_grad, router_grad, table_grad, *gains = pl.pallas_call(
        finish_kernel,
        grid=(steps,),
        in_specs=[
            whole((total, width)),
            slab(count, 1),
            slab(count, 1),
            slab(count, width),
            slab(width, units),
            slab(units, width),
            matrix,
            matrix,
            matrix,
            matrix,
            whole(small_shape),
        ],
        out_specs=[
            slab(count, width),
            slab(width, units),
            slab(units, width),
            matrix,
            matrix,
            matrix,
            matrix,
            whole((experts, width)),
            whole((HEADS, BUCKETS)),
            whole((1, width)),
            whole((1, width)),
        ],
        out_shape=[
            shape((count, width), bf16),
            shape((width, units), f32),
            shape((units, width), f32),
        ]
        + [shape((width, width), f32)] * 4
        + [shape((experts, width), f32), shape((HEADS, BUCKETS), f32)]
        + [shape((1, width), f32)] * 2,
        compiler_params=params,
        name="finish",
    )(
        returned.reshape(total, width),
        target_column,
        gate,
        hidden,
        up_grad,
        down_grad,
        query_grad,
        key_grad,
        value_grad,
        out_grad,
        small,
    )
    return (
        output,
        tokens_grad,
        gains[0].reshape(width),
        query_grad,
        key_grad,
        value_grad,
        out_grad,
        table_grad.T,
        gains[1].reshape(width),
        router_grad.T,
        up_grad[None],
        down_grad[None],
    )


def solution(mesh):
    split = P(BOTH, None)
    experts = P(BOTH, None, None)
    in_specs = (split, P(), P(), P(), P(), P(), P(), P(), P(), experts, experts, split, split)
    out_specs = (split, split, P(), P(), P(), P(), P(), P(), P(), P(), experts, experts)
    return jax.shard_map(local, mesh=mesh, in_specs=in_specs, out_specs=out_specs, check_vma=False)
```

```python
import functools

import jax
import jax.numpy as jnp
import numpy as np
from jax import lax
from jax.experimental import pallas as pl
from jax.experimental.pallas import tpu as pltpu
from jax.sharding import PartitionSpec as P

HEADS = 12
HEAD_DIM = 64
BUCKETS = 32
SEQ_LEN = 512
EPSILON = 1e-06
LIMITS = (12, 16, 23, 32, 46, 64, 91)
HIGHEST = lax.Precision.HIGHEST
MESH = pl.DeviceIdType.MESH
BOTH = ("wide", "narrow")
GROUP = 4
COLUMNS = GROUP * HEAD_DIM
TILE = 128
SPAN = 512
HALF = 256
PIECE = 256
VMEM_LIMIT = 56 * 2**20

bf16 = jnp.bfloat16
f32 = jnp.float32


def product(left, right, **options):
    return jnp.dot(left, right, preferred_element_type=f32, **options)


def product_left(left, right, **options):
    return lax.dot_general(left, right, (((0,), (0,)), ((), ())), preferred_element_type=f32, **options)


def product_right(left, right, **options):
    return lax.dot_general(left, right, (((1,), (1,)), ((), ())), preferred_element_type=f32, **options)


def gelu_curve(values):
    return jax.nn.gelu(values, approximate=True)


def lane_buckets():
    offset = SPAN // 2 - np.arange(SPAN)
    distance = np.abs(offset)
    further = 8 + sum((distance >= limit).astype(np.int32) for limit in LIMITS)
    bucket = np.where(distance < 8, distance, further) + 16 * (offset > 0)
    return (bucket[:, None] == np.arange(BUCKETS)[None, :]).astype(np.float32)


def whole(shape):
    return pl.BlockSpec(shape, lambda *_: (0,) * len(shape))


def find_slots(capacity, experts, row_ref, target_row_ref):
    count = row_ref.shape[1]
    token_down = lax.broadcasted_iota(jnp.int32, (count, count), 0)
    token_across = lax.broadcasted_iota(jnp.int32, (count, count), 1)
    row = row_ref[...]
    picks = row == lax.broadcasted_iota(jnp.int32, (experts, count), 0)
    before = product(picks.astype(bf16), (token_down < token_across).astype(bf16))
    slot = jnp.sum(jnp.where(picks, before, 0.0), axis=0, keepdims=True).astype(jnp.int32)
    target_row_ref[...] = jnp.where(slot < capacity, row * capacity + slot, -1)


def as_column(row):
    return jnp.broadcast_to(row, (8, row.shape[1])).T[:, 0:1]


def place_part(net, part, target_row_ref, rows_ref, sent_ref):
    capacity, width = sent_ref.shape[1:]
    first = net.partner(part, 0)[0] // net.rows * net.length
    size = net.length * capacity
    slots = first * capacity + lax.broadcasted_iota(jnp.int32, (size, rows_ref.shape[0]), 0)
    placing = (slots == target_row_ref[...]).astype(bf16)
    rows = product(placing, rows_ref[...]).astype(bf16)
    sent_ref[pl.ds(first, net.length)] = rows.reshape(net.length, capacity, width)


def forward_kernel(
    n_wide,
    n_narrow,
    groups,
    cotangent_ref,
    tokens_ref,
    gain_one_ref,
    w_query_ref,
    w_key_ref,
    w_value_ref,
    w_out_ref,
    table_ref,
    buckets_ref,
    gain_two_ref,
    row_ref,
    hidden_ref,
    normed_ref,
    normed_t_ref,
    query_ref,
    key_t_ref,
    value_ref,
    weights_ref,
    mixed_t_ref,
    normed_two_ref,
    target_column_ref,
    target_row_ref,
    upstream_ref,
    curves,
    far_s,
    key_rows,
    query_t,
    value_t,
    sent_s,
    send,
    receive,
    own_sem,
):
    group = pl.program_id(0)
    count, width = tokens_ref.shape
    experts, capacity = upstream_ref.shape[:2]
    sequences = count // SEQ_LEN
    net = Exchange(n_wide, n_narrow)
    own_copy = pltpu.make_async_copy(sent_s.at[net.me], upstream_ref.at[net.place], own_sem)

    @pl.when(group == 0)
    def _():
        net.announce()
        find_slots(capacity, experts, row_ref, target_row_ref)
        for turn, part in enumerate(ISSUE):
            if part < net.parts:
                place_part(net, part, target_row_ref, cotangent_ref, sent_s)
                if turn == 0:
                    net.greet()
                net.start_out(sent_s, upstream_ref, send, receive, part)
        own_copy.start()
        target_column_ref[...] = as_column(target_row_ref[...])
        inputs = tokens_ref[...].astype(f32)
        factor = lax.rsqrt(jnp.mean(inputs * inputs, axis=1, keepdims=True) + EPSILON)
        normed = (inputs * factor * gain_one_ref[...].reshape(1, width)).astype(bf16)
        normed_ref[...] = normed
        normed_t_ref[...] = normed.T
        hidden_ref[...] = inputs
        curve = lax.dot_general(
            table_ref[...], buckets_ref[...], (((1,), (1,)), ((), ())), preferred_element_type=f32, precision=HIGHEST
        )
        for head in range(HEADS):
            wide = jnp.broadcast_to(curve[head : head + 1, :], (TILE, SPAN))
            curves[head] = pltpu.roll(wide, 0, 1, stride=1, stride_axis=0)
            far_s[head, 0:1, :] = jnp.broadcast_to(curve[head : head + 1, SPAN - 1 : SPAN], (1, TILE))
            far_s[head, 1:2, :] = jnp.broadcast_to(curve[head : head + 1, 0:1], (1, TILE))

    normed = normed_ref[...]
    query = product(normed, w_query_ref[...]).astype(bf16)
    query_ref[...] = query
    query_t[...] = (query * jnp.asarray(HEAD_DIM**-0.5, bf16)).T
    key = product(normed, w_key_ref[...]).astype(bf16)
    key_rows[...] = key
    key_t_ref[...] = key.T
    value = product(normed, w_value_ref[...]).astype(bf16)
    value_ref[...] = value
    value_t[...] = value.T

    lane = lax.broadcasted_iota(jnp.int32, (SEQ_LEN, TILE), 1)
    for head in range(GROUP):
        pair = head // 2 * TILE
        mine = (lane // HEAD_DIM) == head % 2
        index = group * GROUP + head
        far_left = far_s[index, 0:1, :]
        far_right = far_s[index, 1:2, :]
        for sequence in range(sequences):
            rows = pl.ds(sequence * SEQ_LEN, SEQ_LEN)
            keys = jnp.where(mine, key_rows[rows, pair : pair + TILE], jnp.zeros((), bf16))
            for half in range(SEQ_LEN // HALF):
                columns = pl.ds(sequence * SEQ_LEN + half * HALF, HALF)
                raw = product(keys, query_t[pair : pair + TILE, columns])
                parts = []
                for down in range(SEQ_LEN // TILE):
                    line = []
                    for across in range(HALF // TILE):
                        step = down - (half * (HALF // TILE) + across)
                        block = raw[down * TILE : (down + 1) * TILE, across * TILE : (across + 1) * TILE]
                        if abs(step) <= 1:
                            begin = SPAN // 2 - step * TILE
                            bias = curves[index, :, begin : begin + TILE]
                        else:
                            bias = far_right if step > 0 else far_left
                        line.append(block + bias)
                    parts.append(jnp.concatenate(line, axis=1))
                scores = jnp.concatenate(parts, axis=0)
                maximum = jnp.max(scores, axis=0, keepdims=True)
                exponent = jnp.exp(scores - maximum)
                total = jnp.sum(exponent, axis=0, keepdims=True)
                weights = (exponent * (1.0 / total)).astype(bf16)
                weights_ref[head, sequence, :, half * HALF : (half + 1) * HALF] = weights
                mixed_t_ref[head * HEAD_DIM : (head + 1) * HEAD_DIM, columns] = product(
                    value_t[head * HEAD_DIM : (head + 1) * HEAD_DIM, rows], weights
                ).astype(bf16)
    hidden_ref[...] += product(mixed_t_ref[...].T, w_out_ref[...])

    @pl.when(group == pl.num_programs(0) - 1)
    def _():
        hidden = hidden_ref[...]
        factor = lax.rsqrt(jnp.mean(hidden * hidden, axis=1, keepdims=True) + EPSILON)
        normed_two_ref[...] = (hidden * factor * gain_two_ref[...].reshape(1, width)).astype(bf16)
        own_copy.wait()
        for part in range(net.parts):
            net.wait_out(sent_s, upstream_ref, send, receive, part)
            net.wait_arrivals(upstream_ref, send, receive, part)


def norm_back(values, gain, upstream):
    factor = lax.rsqrt(jnp.mean(values * values, axis=-1, keepdims=True) + EPSILON)
    plain = values * factor
    scaled = upstream * gain
    inner = jnp.mean(scaled * plain, axis=-1, keepdims=True)
    return factor * (scaled - plain * inner), jnp.sum(upstream * plain, axis=0, keepdims=True)


def small_rows(experts):
    return experts, experts + 16, experts + 17, -(-(experts + 18) // 64) * 64


def backward_kernel(
    n_wide,
    n_narrow,
    groups,
    near_ref,
    produced_ref,
    returned_bar_ref,
    gate_lines_ref,
    target_ref,
    row_ref,
    hidden_ref,
    cotangent_ref,
    probs_ref,
    gate_ref,
    gain_two_ref,
    w_router_ref,
    mixed_t_ref,
    w_out_ref,
    tokens_ref,
    gain_one_ref,
    query_ref,
    key_t_ref,
    value_ref,
    weights_ref,
    normed_t_ref,
    w_query_ref,
    w_key_ref,
    w_value_ref,
    buckets_ref,
    *refs,
):
    plans = plans_of(n_wide, n_narrow, groups)
    parts = len(plans)
    returned_ref, result_ref, refs = refs[0], refs[1], refs[2:]
    outs, refs = refs[: THIRDS + 2], refs[THIRDS + 2 :]
    buffers, refs = refs[:parts], refs[parts:]
    sums, refs = refs[:parts], refs[parts:]
    works = []
    for part in range(parts):
        stages, lane_bit = plans[part]
        received, refs = refs[: len(stages)], refs[len(stages) :]
        works.append(Reduction(buffers[part], sums[part], received, refs[0], refs[1], stages, lane_bit))
        refs = refs[2:]
    (
        hidden_bar,
        tokens_grad_ref,
        mixed_bar,
        mixed_bar_t,
        normed_bar,
        scores_s,
        query_bar_t,
        query_rows,
        key_bar,
        value_bar,
        near,
        far,
        diagonals,
        chosen_s,
        back_send,
        back_receive,
        own_sems,
    ) = refs
    hidden_low = tokens_grad_ref
    group = pl.program_id(0)
    count, width = normed_bar.shape
    experts, capacity = produced_ref.shape[:2]
    total = experts * capacity
    sequences = count // SEQ_LEN
    scale = HEAD_DIM**-0.5
    net = Exchange(n_wide, n_narrow)
    router_end, gain_two_at, gain_one_at, _ = small_rows(experts)
    near_blocks = pl.ds(net.top * net.length, NEAR * net.length)
    own_copy = pltpu.make_async_copy(near_ref.at[near_blocks], returned_ref.at[near_blocks], own_sems.at[0])
    hidden_copy = pltpu.make_async_copy(hidden_ref, hidden_bar, own_sems.at[1])
    cotangent_copy = pltpu.make_async_copy(cotangent_ref, tokens_grad_ref, own_sems.at[2])
    tokens_copy = pltpu.make_async_copy(tokens_ref, mixed_bar, own_sems.at[3])
    small = buffers[-1]

    def give_back(turn):
        if turn < len(ISSUE) and NEAR <= ISSUE[turn] < net.parts:
            net.start_back(produced_ref, returned_ref, back_send, back_receive, ISSUE[turn])

    @pl.when(group == 0)
    def _():
        net.announce()
        hidden_copy.start()
        cotangent_copy.start()
        net.greet()
        give_back(0)
        own_copy.start()
        diagonals[...] = jnp.zeros_like(diagonals)
        small[...] = jnp.zeros_like(small)
        hidden_copy.wait()
        cotangent_copy.wait()

        chosen_s[...] = as_column(row_ref[...])

        def prologue(index, carry):
            rows = pl.ds(pl.multiple_of(index * PIECE, PIECE), PIECE)
            target = target_ref[rows, :]
            chosen = chosen_s[rows, :]
            placing = (target == lax.broadcasted_iota(jnp.int32, (PIECE, total), 1)).astype(bf16)
            normed_two_bar = product(placing, returned_bar_ref[...])
            picks = chosen == lax.broadcasted_iota(jnp.int32, (PIECE, experts), 1)
            lines = product(picks.astype(f32), gate_lines_ref[...], precision=HIGHEST)
            slots = (target - chosen * capacity) == lax.broadcasted_iota(jnp.int32, (PIECE, 128), 1)
            gate_bar = jnp.sum(jnp.where(slots, lines, 0.0), axis=1, keepdims=True)
            inner = gate_ref[rows, :] * gate_bar
            logits_bar = (probs_ref[rows, :] * (jnp.where(picks, gate_bar, 0.0) - inner)).astype(bf16)
            normed_two_bar = normed_two_bar + product(logits_bar, w_router_ref[...])
            hidden = hidden_bar[rows, :]
            factor = lax.rsqrt(jnp.mean(hidden * hidden, axis=1, keepdims=True) + EPSILON)
            normed_two = (hidden * factor * gain_two_ref[...].reshape(1, width)).astype(bf16)
            small[0:router_end, :] += product_left(logits_bar, normed_two)
            back, gain_part = norm_back(hidden, gain_two_ref[...].reshape(1, width), normed_two_bar)
            small[gain_two_at : gain_two_at + 1, :] += gain_part
            bar = tokens_grad_ref[rows, :].astype(f32) + back
            hidden_bar[rows, :] = bar
            low = bar.astype(bf16)
            hidden_low[rows, :] = low
            mixed_bar[rows, :] = product_right(low, w_out_ref[...]).astype(bf16)
            return carry

        lax.fori_loop(0, count // PIECE, prologue, 0)
        for third in range(THIRDS):
            columns = pl.ds(third * COLUMNS, COLUMNS)
            buffers[third][...] = product(mixed_t_ref[...], hidden_low[:, columns]).astype(bf16)
            works[third].start(0)
        mixed_bar_t[...] = product_right(w_out_ref[...], hidden_low[...]).astype(bf16)

    def tick(head):
        for now in range(groups):
            turn = now * GROUP + head
            active = [(part, turns.index(turn)) for part, turns in enumerate(ADVANCE) if turn in turns]
            sends = [index + 1 for index, at in enumerate(GIVE) if at == turn]

            @pl.when(group == now)
            def _(active=active, sends=sends):
                for index in sends:
                    give_back(index)
                for job, step in active:
                    for part in range(job * THIRDS, (job + 1) * THIRDS):
                        works[part].finish(step)
                        works[part].start(step + 1)

    lane = lax.broadcasted_iota(jnp.int32, (SEQ_LEN, TILE), 1)
    features = pl.ds(pl.multiple_of(group * COLUMNS, COLUMNS), COLUMNS)
    for head in range(GROUP):
        pair = pl.ds(pl.multiple_of(group * COLUMNS + head // 2 * TILE, TILE), TILE)
        local_pair = pl.ds(head // 2 * TILE, TILE)
        mine = (lane // HEAD_DIM) == head % 2
        feature = pl.ds(head * HEAD_DIM, HEAD_DIM)
        near[...] = jnp.zeros_like(near)
        far[...] = jnp.zeros_like(far)
        for sequence in range(sequences):
            rows = pl.ds(sequence * SEQ_LEN, SEQ_LEN)
            values = jnp.where(mine, value_ref[rows, local_pair], jnp.zeros((), bf16))
            for half in range(SEQ_LEN // HALF):
                columns = pl.ds(sequence * SEQ_LEN + half * HALF, HALF)
                probs_bar = product(values, mixed_bar_t[pair, columns])
                probs = weights_ref[head, sequence, :, half * HALF : (half + 1) * HALF].astype(f32)
                shared = probs * probs_bar
                summed = jnp.sum(shared, axis=0, keepdims=True)
                scores_bar = shared - probs * summed
                scores_s[:, half * HALF : (half + 1) * HALF] = scores_bar.astype(bf16)
                for down in range(SEQ_LEN // TILE):
                    for across in range(HALF // TILE):
                        step = down - (half * (HALF // TILE) + across)
                        block = scores_bar[down * TILE : (down + 1) * TILE, across * TILE : (across + 1) * TILE]
                        if abs(step) <= 1:
                            begin = SPAN // 2 - step * TILE
                            near[:, begin : begin + TILE] += block
                        else:
                            side = 1 if step > 0 else 0
                            far[side] += jnp.sum(block.reshape(TILE // 8, 8, TILE), axis=0)
            weights = weights_ref[head, sequence]
            scores_low = scores_s[...]
            value_part = product(weights, mixed_bar[rows, pair]).astype(bf16)
            key_part = (product(scores_low, query_ref[rows, local_pair]) * scale).astype(bf16)
            if head % 2 == 0:
                value_bar[rows, local_pair] = value_part
                key_bar[rows, local_pair] = key_part
            else:
                value_bar[rows, local_pair] = jnp.where(mine, value_part, value_bar[rows, local_pair])
                key_bar[rows, local_pair] = jnp.where(mine, key_part, key_bar[rows, local_pair])
            query_bar_t[feature, rows] = (product(key_t_ref[feature, rows], scores_low) * scale).astype(bf16)
        folded = near[0:8, :]
        for step in range(1, TILE // 8):
            folded = folded + pltpu.roll(near[8 * step : 8 * step + 8, :], SPAN - 8 * step, 1)
        place = lax.broadcasted_iota(jnp.int32, (8, SPAN), 0)
        for bit in (4, 2, 1):
            folded = jnp.where((place & bit) > 0, pltpu.roll(folded, SPAN - bit, 1), folded)
        gathered = jnp.sum(folded, axis=0, keepdims=True)
        place = lax.broadcasted_iota(jnp.int32, (1, SPAN), 1)
        left = jnp.sum(far[0])
        right = jnp.sum(far[1])
        gathered = gathered + jnp.where(place == SPAN - 1, left, 0.0) + jnp.where(place == 0, right, 0.0)
        diagonals[pl.ds(group * GROUP + head, 1), :] = gathered
        tick(head)

    @pl.when(group == groups - 1)
    def _():
        tokens_copy.start()

    query_bar = query_bar_t[...].T
    normed_t = normed_t_ref[...]
    query_rows[...] = query_bar
    for now in range(groups):

        @pl.when(group == now)
        def _(now=now):
            for index, part in enumerate((query_rows, key_bar, value_bar)):
                place = (now + 1) * THIRDS + index
                buffers[place][...] = product(normed_t, part[...]).astype(bf16)
                works[place].start(0)


    def project(index, carry):
        rows = pl.ds(pl.multiple_of(index * PIECE, PIECE), PIECE)
        bar = (
            product_right(query_rows[rows, :], w_query_ref[...])
            + product_right(key_bar[rows, :], w_key_ref[...])
            + product_right(value_bar[rows, :], w_value_ref[...])
        )

        @pl.when(group == 0)
        def _():
            normed_bar[rows, :] = bar

        @pl.when(group > 0)
        def _():
            normed_bar[rows, :] += bar

        @pl.when(group == groups - 1)
        def _():
            back, gain_part = norm_back(mixed_bar[rows, :].astype(f32), gain_one_ref[...].reshape(1, width), normed_bar[rows, :])
            tokens_grad_ref[rows, :] = (hidden_bar[rows, :] + back).astype(bf16)
            small[gain_one_at : gain_one_at + 1, :] += gain_part

        return carry

    @pl.when(group == groups - 1)
    def _():
        tokens_copy.wait()

    lax.fori_loop(0, count // PIECE, project, 0)

    @pl.when(group == groups - 1)
    def _():
        small[router_end : router_end + 16, 0:BUCKETS] = product(
            diagonals[...], buckets_ref[...], precision=HIGHEST
        )
        works[-1].start(0)
        outward = []
        for part in range(parts):
            job, third = divmod(part, THIRDS)
            if part == parts - 1:
                goal = outs[-1]
            elif job == 0:
                goal = outs[THIRDS].at[:, pl.ds(third * COLUMNS, COLUMNS)]
            else:
                goal = outs[third].at[:, pl.ds((job - 1) * COLUMNS, COLUMNS)]
            outward.append(pltpu.make_async_copy(sums[part], goal, own_sems.at[5 + part]))
        outward.append(pltpu.make_async_copy(tokens_grad_ref, result_ref, own_sems.at[4]))
        outward[-1].start()
        at = [len(turns) for turns in ADVANCE for _ in range(THIRDS)] + [0]
        while any(step < work.steps for step, work in zip(at, works)):
            for part, work in enumerate(works):
                work.finish(at[part])
                work.start(at[part] + 1)
                at[part] += 1
                if at[part] == work.steps:
                    outward[part].start()
        for copy in outward:
            copy.wait()
        own_copy.wait()
        for part in range(NEAR, net.parts):
            net.wait_back(produced_ref, returned_ref, back_send, back_receive, part)
        net.wait_returns(returned_ref, back_send, back_receive, range(NEAR, net.parts))


def plan_of(n_wide, n_narrow, halvings, turn, size):
    bits = [("narrow", 1 << b) for b in range(n_narrow.bit_length() - 1)]
    bits += [("wide", 1 << b) for b in range(n_wide.bit_length() - 1)]
    if turn and len(bits) > 2:
        bits[1], bits[2] = bits[2], bits[1]
    stages, done = [], 0
    while done < len(bits):
        halve = done < halvings
        many = min(size if done >= 3 else 1, (halvings if halve else len(bits)) - done)
        stages.append((tuple(bits[done : done + many]), halve))
        done += many
    return stages, bits[0]


THIRDS = 3


def plans_of(n_wide, n_narrow, groups):
    plans = []
    for job in range(groups + 1):
        for third in range(THIRDS):
            plans.append(plan_of(n_wide, n_narrow, 5, (third + job) % 2, LAST if job == groups else OTHERS))
    return plans + [plan_of(n_wide, n_narrow, 3, 0, 2)]


class Reduction:
    def __init__(self, buffer, gathered, received, send, receive, stages, lane_bit):
        self.buffer, self.gathered, self.received = buffer, gathered, received
        self.send, self.receive = send, receive
        self.stages, self.lane_bit = stages, lane_bit
        self.place = {"wide": lax.axis_index("wide"), "narrow": lax.axis_index("narrow")}
        rows, lanes = buffer.shape
        self.regions = [((0, rows), (0, lanes))]
        for bits, halve in stages:
            region = self.regions[-1]
            self.regions.append(self.piece(region, bits, 0) if halve else region)
        self.back = [index for index, (_, halve) in enumerate(stages) if halve][::-1]
        self.steps = len(stages) + len(self.back)
        self.first = [0]
        for step in range(self.steps):
            self.first.append(self.first[-1] + self.others(step) )

    def stage_of(self, step):
        return step if step < len(self.stages) else self.back[step - len(self.stages)]

    def others(self, step):
        return 2 ** len(self.stages[self.stage_of(step)][0]) - 1

    def own(self, bit):
        return (self.place[bit[0]] // bit[1]) % 2

    def piece(self, region, bits, change):
        (row, rows), (lane, lanes) = region
        for index, bit in enumerate(bits):
            own = self.own(bit)
            if (change >> index) & 1:
                own = 1 - own
            if bit == self.lane_bit:
                lanes = lanes // 2
                lane = lane + own * lanes
            else:
                rows = rows // 2
                row = row + own * rows
        return (row, rows), (lane, lanes)

    def target(self, bits, change):
        place = dict(self.place)
        for index, bit in enumerate(bits):
            if (change >> index) & 1:
                place[bit[0]] = place[bit[0]] + bit[1] - 2 * bit[1] * self.own(bit)
        return place["wide"], place["narrow"]

    def view(self, buffer, region):
        (row, rows), (lane, lanes) = region
        row = row if isinstance(row, int) else pl.multiple_of(row, 16 if self.buffer.dtype == bf16 else 8)
        lane = lane if isinstance(lane, int) else pl.multiple_of(lane, 128)
        return buffer.at[pl.ds(row, rows), pl.ds(lane, lanes)]

    def copy(self, step, change):
        stage = self.stage_of(step)
        bits, halve = self.stages[stage]
        if step < len(self.stages):
            region = self.piece(self.regions[stage], bits, change) if halve else self.regions[stage]
            source, sink = self.view(self.buffer, region), self.received[stage].at[change - 1]
        else:
            source = sink = self.view(self.gathered, self.regions[stage + 1])
        index = self.first[step] + change - 1
        return pltpu.make_async_remote_copy(
            src_ref=source,
            dst_ref=sink,
            send_sem=self.send.at[index],
            recv_sem=self.receive.at[index],
            device_id=self.target(bits, change),
            device_id_type=MESH,
        )

    def start(self, step):
        if 0 <= step < self.steps:
            for change in range(1, self.others(step) + 1):
                self.copy(step, change).start()

    def finish(self, step):
        if not 0 <= step < self.steps:
            return
        for change in range(1, self.others(step) + 1):
            self.copy(step, change).wait()
        if step < len(self.stages):
            region = self.regions[step + 1]
            mine = self.view(self.buffer, region)
            result = mine if step < len(self.stages) - 1 else self.view(self.gathered, region)
            total = mine[...].astype(f32)
            for change in range(self.others(step)):
                total = total + self.received[step][change].astype(f32)
            result[...] = total.astype(mine.dtype)


def reduction_scratch(shape, dtype, stages, lane_bit):
    rows, lanes = shape
    received, copies = [], 0
    for bits, halve in stages:
        if halve:
            for bit in bits:
                if bit == lane_bit:
                    lanes //= 2
                else:
                    rows //= 2
        others = 2 ** len(bits) - 1
        received.append(pltpu.VMEM((others, rows, lanes), dtype))
        copies += others * (2 if halve else 1)
    return received, copies


class Exchange:
    def __init__(self, n_wide, n_narrow):
        self.n_wide, self.n_narrow = n_wide, n_narrow
        self.count = n_wide * n_narrow
        self.parts = min(4, n_wide)
        self.rows = n_wide // self.parts
        self.length = self.rows * n_narrow
        w, k = lax.axis_index("wide"), lax.axis_index("narrow")
        self.me = w * n_narrow + k
        self.top, self.place = w // self.rows, (w % self.rows) * n_narrow + k

    def partner(self, part, place):
        top, bit = self.top, 1
        while bit < self.parts:
            if part & bit:
                top = top + bit - 2 * bit * ((top // bit) % 2)
            bit *= 2
        w = top * self.rows + place // self.n_narrow
        return w, place % self.n_narrow

    def each(self, part, act):
        def body(place, carry):
            if part == 0:

                @pl.when(place != self.place)
                def _():
                    act(place)

            else:
                act(place)
            return carry

        lax.fori_loop(0, self.length, body, 0)

    def announce(self):
        barrier = pltpu.get_barrier_semaphore()
        for part in range(self.parts):

            def act(place, part=part):
                pl.semaphore_signal(barrier, inc=1, device_id=self.partner(part, place), device_id_type=MESH)

            self.each(part, act)

    def greet(self):
        pl.semaphore_wait(pltpu.get_barrier_semaphore(), self.count - 1)

    def out(self, source, sink, send, receive, part, place):
        w, k = self.partner(part, place)
        slot = part * self.length
        return pltpu.make_async_remote_copy(
            src_ref=source.at[w * self.n_narrow + k],
            dst_ref=sink.at[slot + self.place],
            send_sem=send.at[slot + place],
            recv_sem=receive.at[slot + self.place],
            device_id=(w, k),
            device_id_type=MESH,
        )

    def back(self, source, sink, send, receive, part, place):
        slot = part * self.length + place
        return pltpu.make_async_remote_copy(
            src_ref=source.at[slot],
            dst_ref=sink.at[self.me],
            send_sem=send.at[slot],
            recv_sem=receive.at[self.me],
            device_id=self.partner(part, place),
            device_id_type=MESH,
        )

    def arrival(self, sink, send, receive, slot):
        return pltpu.make_async_remote_copy(
            src_ref=sink.at[slot],
            dst_ref=sink.at[slot],
            send_sem=send.at[slot],
            recv_sem=receive.at[slot],
            device_id=self.partner(self.parts - 1, self.place),
            device_id_type=MESH,
        )

    def start_out(self, source, sink, send, receive, part):
        self.each(part, lambda place: self.out(source, sink, send, receive, part, place).start())

    def wait_out(self, source, sink, send, receive, part):
        self.each(part, lambda place: self.out(source, sink, send, receive, part, place).wait_send())

    def wait_arrivals(self, sink, send, receive, part):
        slot = part * self.length
        self.each(part, lambda place: self.arrival(sink, send, receive, slot + place).wait_recv())

    def start_back(self, source, sink, send, receive, part):
        self.each(part, lambda place: self.back(source, sink, send, receive, part, place).start())

    def wait_back(self, source, sink, send, receive, part):
        self.each(part, lambda place: self.back(source, sink, send, receive, part, place).wait_send())

    def wait_returns(self, sink, send, receive, parts):
        for part in parts:
            first = self.partner(part, 0)[0] // self.rows * self.length

            def act(place, first=first):
                self.arrival(sink, send, receive, first + place).wait_recv()

            self.each(part, act)


NEAR = 1
ISSUE = (2, 3, 1, 0)
ADVANCE = ((3, 7, 11), (7, 11), (11,), ())
OTHERS, LAST = 2, 2
GIVE = (3, 7)


def experts_kernel(
    n_wide,
    n_narrow,
    target_row_ref,
    row_ref,
    normed_two_ref,
    w_router_ref,
    upstream_ref,
    w_up_ref,
    w_down_ref,
    probs_ref,
    gate_ref,
    back_ref,
    gate_back_ref,
    near_ref,
    produced_ref,
    up_grad_ref,
    down_grad_ref,
    sent_ref,
    rows_s,
    upstream_s,
    w_up_s,
    w_down_s,
    active_s,
    bar_s,
    rows_bar_s,
    produced_s,
    gate_s,
    scaled_s,
    rows_t_s,
    stage_s,
    send,
    receive,
    back_send,
    back_receive,
    gate_send,
    gate_receive,
    near_send,
    near_receive,
    local_sems,
):
    net = Exchange(n_wide, n_narrow)
    count, capacity, width = rows_s.shape
    length = net.length
    piece = length * capacity
    hidden_units = w_up_s.shape[1]
    tile = min(768, hidden_units)
    tiles = hidden_units // tile
    net.announce()
    down_copy = pltpu.make_async_copy(w_down_ref, w_down_s, local_sems.at[0])
    down_copy.start()
    upstream_copy = pltpu.make_async_copy(upstream_ref, upstream_s, local_sems.at[1])
    upstream_copy.start()
    up_copy = pltpu.make_async_copy(w_up_ref, w_up_s, local_sems.at[2])
    up_copy.start()
    own_copy = pltpu.make_async_copy(sent_ref.at[net.me], rows_s.at[net.place], local_sems.at[3])
    for turn, part in enumerate(ISSUE):
        if part < net.parts:
            place_part(net, part, target_row_ref, normed_two_ref, sent_ref)
            if turn == 0:
                net.greet()
            net.start_out(sent_ref, rows_s, send, receive, part)
    own_copy.start()
    down_copy.wait()
    upstream_copy.wait()

    def before(index, carry):
        part, span = index // tiles, index % tiles
        units = pl.ds(pl.multiple_of(span * tile, tile), tile)
        upstream = upstream_s[pl.ds(part * length, length)].reshape(piece, width)
        bar_s[part, :, units] = product_right(upstream, w_down_s[units, :]).astype(bf16)
        return carry

    lax.fori_loop(0, net.parts * tiles, before, 0)
    up_copy.wait()
    own_copy.wait()
    for part in (0, 2, 1, 3):
        net.wait_arrivals(rows_s, send, receive, part)
        blocks = pl.ds(part * length, length)
        rows = rows_s[blocks].reshape(piece, width)
        upstream = upstream_s[blocks].reshape(piece, width).astype(f32)
        logits = product_right(rows, w_router_ref[...])
        exponent = jnp.exp(logits - jnp.max(logits, axis=1, keepdims=True))
        probs = exponent / jnp.sum(exponent, axis=1, keepdims=True)
        mine = lax.broadcasted_iota(jnp.int32, probs.shape, 1) == net.me
        gate = jnp.sum(jnp.where(mine, probs, 0.0), axis=1, keepdims=True)
        scaled_s[part * piece : (part + 1) * piece, :] = (gate * upstream).astype(bf16)

        def through(span, carry):
            produced, rows_bar = carry
            units = pl.ds(pl.multiple_of(span * tile, tile), tile)
            raised = product(rows, w_up_s[:, units])
            square = raised * raised
            inner = raised * (0.7978845608028654 + 0.7978845608028654 * 0.044715 * square)
            half = 0.5 + 0.5 * jnp.tanh(inner)
            active = (raised * half).astype(bf16)
            active_s[part * piece : (part + 1) * piece, units] = active
            slope = half + 2.0 * raised * half * (1.0 - half) * (
                0.7978845608028654 + 3.0 * 0.7978845608028654 * 0.044715 * square
            )
            raised_bar = (gate * bar_s[part, :, units].astype(f32) * slope).astype(bf16)
            bar_s[part, :, units] = raised_bar
            rows_bar = rows_bar + product_right(raised_bar, w_up_s[:, units])
            produced = produced + product(active, w_down_s[units, :])
            return produced, rows_bar

        zeros = jnp.zeros((piece, width), f32)
        produced, rows_bar = lax.fori_loop(0, tiles, through, (zeros, zeros))
        rows_bar_s[blocks] = rows_bar.astype(bf16).reshape(length, capacity, width)
        net.start_back(rows_bar_s, back_ref, back_send, back_receive, part)
        produced = produced.astype(bf16)
        produced_s[blocks] = produced.reshape(length, capacity, width)
        if part < NEAR:
            net.start_back(produced_s, near_ref, near_send, near_receive, part)
        gate_bar = jnp.sum(upstream * produced.astype(f32), axis=1, keepdims=True)
        slot = lax.broadcasted_iota(jnp.int32, (length, capacity, 128), 1)
        lane = lax.broadcasted_iota(jnp.int32, (length, capacity, 128), 2)
        spread = jnp.broadcast_to(gate_bar, (piece, 128)).reshape(length, capacity, 128)
        line = jnp.sum(jnp.where(slot == lane, spread, 0.0), axis=1, keepdims=True)
        gate_s[blocks] = jnp.broadcast_to(line, (length, 8, 128))
        net.start_back(gate_s, gate_back_ref, gate_send, gate_receive, part)
    logits = product_right(normed_two_ref[...], w_router_ref[...])
    exponent = jnp.exp(logits - jnp.max(logits, axis=1, keepdims=True))
    probs = exponent / jnp.sum(exponent, axis=1, keepdims=True)
    probs_ref[...] = probs
    picks = as_column(row_ref[...]) == lax.broadcasted_iota(jnp.int32, probs.shape, 1)
    gate_ref[...] = jnp.sum(jnp.where(picks, probs, 0.0), axis=1, keepdims=True)
    own_back = pltpu.make_async_copy(rows_bar_s.at[net.place], back_ref.at[net.me], local_sems.at[0])
    own_back.start()
    own_gate = pltpu.make_async_copy(gate_s.at[net.place], gate_back_ref.at[net.me], local_sems.at[1])
    own_gate.start()
    made = pltpu.make_async_copy(produced_s, produced_ref, local_sems.at[2])
    made.start()
    own_near = pltpu.make_async_copy(produced_s.at[net.place], near_ref.at[net.me], local_sems.at[3])
    own_near.start()
    total = count * capacity
    rows_t_s[...] = rows_s[...].reshape(total, width).T
    copies = [None, None]
    for span in range(2 * tiles):
        side = span % 2
        units = pl.ds((span // 2) * tile, tile)
        if copies[side] is not None:
            copies[side].wait()
        if side == 0:
            bar = bar_s[:, :, units].reshape(total, tile)
            stage_s[side] = product(rows_t_s[...], bar).astype(bf16)
            goal = up_grad_ref.at[:, units]
        else:
            active_t = active_s[:, units].T
            stage_s[side] = product(active_t, scaled_s[...]).astype(bf16)
            goal = down_grad_ref.at[units, :]
        copies[side] = pltpu.make_async_copy(stage_s.at[side], goal, local_sems.at[4 + side])
        copies[side].start()
    for copy in copies:
        copy.wait()
    own_back.wait()
    own_gate.wait()
    made.wait()
    own_near.wait()
    for part in range(net.parts):
        net.wait_out(sent_ref, rows_s, send, receive, part)
        if part < NEAR:
            net.wait_back(produced_s, near_ref, near_send, near_receive, part)
        net.wait_back(rows_bar_s, back_ref, back_send, back_receive, part)
        net.wait_back(gate_s, gate_back_ref, gate_send, gate_receive, part)
    net.wait_returns(back_ref, back_send, back_receive, range(net.parts))
    net.wait_returns(gate_back_ref, gate_send, gate_receive, range(net.parts))
    net.wait_returns(near_ref, near_send, near_receive, range(NEAR))


def run_experts(n_wide, n_narrow, target_row, routes, normed_two, w_router, upstream, w_up, w_down):
    count, capacity, width = upstream.shape
    tokens, experts = normed_two.shape[0], w_router.shape[0]
    units = w_up.shape[1]
    total = count * capacity
    parts = min(4, n_wide)
    tile = min(768, units)
    dma = pltpu.SemaphoreType.DMA
    any_space = pl.BlockSpec(memory_space=pl.ANY)
    shape = jax.ShapeDtypeStruct
    return pl.pallas_call(
        functools.partial(experts_kernel, n_wide, n_narrow),
        out_shape=[
            shape((tokens, experts), f32),
            shape((tokens, 1), f32),
            shape((count, capacity, width), bf16),
            shape((count, 8, 128), f32),
            shape((count, capacity, width), bf16),
            shape((count, capacity, width), bf16),
            shape((width, units), bf16),
            shape((units, width), bf16),
        ],
        in_specs=[pl.BlockSpec(memory_space=pltpu.VMEM)] * 4 + [any_space] * 3,
        out_specs=[pl.BlockSpec(memory_space=pltpu.VMEM)] * 2 + [any_space] * 6,
        scratch_shapes=[
            pltpu.VMEM((count, capacity, width), bf16),
            pltpu.VMEM((count, capacity, width), bf16),
            pltpu.VMEM((count, capacity, width), bf16),
            pltpu.VMEM((width, units), bf16),
            pltpu.VMEM((units, width), bf16),
            pltpu.VMEM((total, units), bf16),
            pltpu.VMEM((parts, total // parts, units), bf16),
            pltpu.VMEM((count, capacity, width), bf16),
            pltpu.VMEM((count, capacity, width), bf16),
            pltpu.VMEM((count, 8, 128), f32),
            pltpu.VMEM((total, width), bf16),
            pltpu.VMEM((width, total), bf16),
            pltpu.VMEM((2, tile, max(tile, width)), bf16),
            dma((count,)),
            dma((count,)),
            dma((count,)),
            dma((count,)),
            dma((count,)),
            dma((count,)),
            dma((count,)),
            dma((count,)),
            dma((6,)),
        ],
        compiler_params=pltpu.CompilerParams(collective_id=1, has_side_effects=True, vmem_limit_bytes=VMEM_LIMIT),
        cost_estimate=pl.CostEstimate(flops=36 * 10**9, bytes_accessed=40 * 10**6, transcendentals=4 * 10**6),
        name="experts",
    )(target_row, routes, normed_two, w_router, upstream, w_up, w_down)


def finish_kernel(
    returned_ref,
    target_ref,
    gate_ref,
    hidden_ref,
    up_ref,
    down_ref,
    query_ref,
    key_ref,
    value_ref,
    out_ref,
    small_ref,
    output_ref,
    up_grad_ref,
    down_grad_ref,
    query_grad_ref,
    key_grad_ref,
    value_grad_ref,
    out_grad_ref,
    router_grad_ref,
    table_grad_ref,
    gain_one_grad_ref,
    gain_two_grad_ref,
):
    total = returned_ref.shape[0]
    placing = (target_ref[...] == lax.broadcasted_iota(jnp.int32, (target_ref.shape[0], total), 1)).astype(bf16)
    gathered = product(placing, returned_ref[...])
    output_ref[...] = (hidden_ref[...] + gate_ref[...] * gathered).astype(bf16)
    up_grad_ref[...] = up_ref[...].astype(f32)
    down_grad_ref[...] = down_ref[...].astype(f32)
    query_grad_ref[...] = query_ref[...].astype(f32)
    key_grad_ref[...] = key_ref[...].astype(f32)
    value_grad_ref[...] = value_ref[...].astype(f32)
    out_grad_ref[...] = out_ref[...].astype(f32)

    @pl.when(pl.program_id(0) == 0)
    def _():
        experts = router_grad_ref.shape[0]
        router_end, gain_two_at, gain_one_at, _ = small_rows(experts)
        router_grad_ref[...] = small_ref[0:router_end, :]
        table_grad_ref[...] = small_ref[router_end : router_end + HEADS, 0:BUCKETS]
        gain_one_grad_ref[...] = small_ref[gain_one_at : gain_one_at + 1, :].reshape(small_ref.shape[1])
        gain_two_grad_ref[...] = small_ref[gain_two_at : gain_two_at + 1, :].reshape(small_ref.shape[1])


def local(
    tokens,
    gain_one,
    w_query,
    w_key,
    w_value,
    w_out,
    table,
    gain_two,
    w_router,
    w_up,
    w_down,
    routes,
    cotangent,
):
    count, width = tokens.shape
    experts = w_router.shape[1]
    n_wide, n_narrow = lax.axis_size("wide"), lax.axis_size("narrow")
    me = lax.axis_index("wide") * n_narrow + lax.axis_index("narrow")
    capacity = max(2, (5 * count + 4 * experts - 1) // (4 * experts))
    total = experts * capacity
    sequences = count // SEQ_LEN
    groups = HEADS // GROUP
    params = pltpu.CompilerParams(vmem_limit_bytes=VMEM_LIMIT)
    routes, w_router = routes.reshape(1, count), w_router.T
    buckets = jnp.asarray(lane_buckets())
    shape = jax.ShapeDtypeStruct

    any_space = pl.BlockSpec(memory_space=pl.ANY)
    dma = pltpu.SemaphoreType.DMA
    columns = pl.BlockSpec((count, COLUMNS), lambda g: (0, g))
    rows_t = pl.BlockSpec((COLUMNS, count), lambda g: (g, 0))
    weight = pl.BlockSpec((width, COLUMNS), lambda g: (0, g))
    weights_block = pl.BlockSpec((GROUP, sequences, SEQ_LEN, SEQ_LEN), lambda g: (g, 0, 0, 0))
    (
        hidden,
        normed_one,
        normed_t,
        query,
        key_t,
        value,
        weights,
        mixed_t,
        normed_two,
        target_column,
        target_row,
        upstream_rows,
    ) = pl.pallas_call(
        functools.partial(forward_kernel, n_wide, n_narrow, groups),
        grid=(groups,),
        in_specs=[
            whole((count, width)),
            whole((count, width)),
            whole((width,)),
            weight,
            weight,
            weight,
            pl.BlockSpec((COLUMNS, width), lambda g: (g, 0)),
            whole((HEADS, BUCKETS)),
            whole((SPAN, BUCKETS)),
            whole((width,)),
            whole((1, count)),
        ],
        out_specs=[
            whole((count, width)),
            whole((count, width)),
            whole((width, count)),
            columns,
            rows_t,
            columns,
            weights_block,
            rows_t,
            whole((count, width)),
            whole((count, 1)),
            whole((1, count)),
            any_space,
        ],
        out_shape=[
            shape((count, width), f32),
            shape((count, width), bf16),
            shape((width, count), bf16),
            shape((count, width), bf16),
            shape((width, count), bf16),
            shape((count, width), bf16),
            shape((HEADS, sequences, SEQ_LEN, SEQ_LEN), bf16),
            shape((width, count), bf16),
            shape((count, width), bf16),
            shape((count, 1), jnp.int32),
            shape((1, count), jnp.int32),
            shape((experts, capacity, width), bf16),
        ],
        scratch_shapes=[
            pltpu.VMEM((HEADS, TILE, SPAN), f32),
            pltpu.VMEM((HEADS, 8, TILE), f32),
            pltpu.VMEM((count, COLUMNS), bf16),
            pltpu.VMEM((COLUMNS, count), bf16),
            pltpu.VMEM((COLUMNS, count), bf16),
            pltpu.VMEM((experts, capacity, width), bf16),
            dma((experts,)),
            dma((experts,)),
            dma,
        ],
        compiler_params=pltpu.CompilerParams(collective_id=2, has_side_effects=True, vmem_limit_bytes=VMEM_LIMIT),
        cost_estimate=pl.CostEstimate(flops=14 * 10**9, bytes_accessed=40 * 10**6, transcendentals=10**7),
        name="attention_forward",
    )(
        cotangent,
        tokens,
        gain_one,
        w_query,
        w_key,
        w_value,
        w_out,
        table.T,
        buckets,
        gain_two,
        routes,
    )

    probs, gate, returned_bar, gate_lines, near, produced, up_grad, down_grad = run_experts(
        n_wide, n_narrow, target_row, routes, normed_two, w_router, upstream_rows, w_up[0], w_down[0]
    )

    def once(block):
        return pl.BlockSpec(block, lambda g: (0,) * len(block), pipeline_mode=pl.Buffered(1))

    plans = plans_of(n_wide, n_narrow, groups)
    *_, small_height = small_rows(experts)
    third = (width, COLUMNS)
    small_shape = (small_height, width)
    part_shapes = [(third, bf16)] * (len(plans) - 1) + [(small_shape, f32)]
    parts = len(part_shapes)
    scratch = [pltpu.VMEM(*part) for part in part_shapes] * 2
    for part, (form, kind) in enumerate(part_shapes):
        received, copies = reduction_scratch(form, kind, *plans[part])
        scratch += received + [pltpu.SemaphoreType.DMA((copies,))] * 2
    returned, tokens_grad, query_grad, key_grad, value_grad, out_grad, small = pl.pallas_call(
        functools.partial(backward_kernel, n_wide, n_narrow, groups),
        grid=(groups,),
        in_specs=[
            any_space,
            any_space,
            once((total, width)),
            once((experts, 128)),
            once((count, 1)),
            once((1, count)),
            any_space,
            any_space,
            once((count, experts)),
            once((count, 1)),
            once((width,)),
            once((experts, width)),
            once((width, count)),
            once((width, width)),
            any_space,
            once((width,)),
            columns,
            rows_t,
            columns,
            weights_block,
            once((width, count)),
            weight,
            weight,
            weight,
            once((SPAN, BUCKETS)),
        ],
        out_specs=[any_space] * (THIRDS + 4),
        out_shape=[shape((experts, capacity, width), bf16), shape((count, width), bf16)]
        + [shape((width, width), bf16)] * (THIRDS + 1)
        + [shape(small_shape, f32)],
        scratch_shapes=scratch
        + [
            pltpu.VMEM((count, width), f32),
            pltpu.VMEM((count, width), bf16),
            pltpu.VMEM((count, width), bf16),
            pltpu.VMEM((width, count), bf16),
            pltpu.VMEM((count, width), f32),
            pltpu.VMEM((SEQ_LEN, SEQ_LEN), bf16),
            pltpu.VMEM((COLUMNS, count), bf16),
            pltpu.VMEM((count, COLUMNS), bf16),
            pltpu.VMEM((count, COLUMNS), bf16),
            pltpu.VMEM((count, COLUMNS), bf16),
            pltpu.VMEM((TILE, SPAN), f32),
            pltpu.VMEM((2, 8, TILE), f32),
            pltpu.VMEM((16, SPAN), f32),
            pltpu.VMEM((count, 1), jnp.int32),
            dma((experts,)),
            dma((experts,)),
            dma((5 + parts,)),
        ],
        compiler_params=pltpu.CompilerParams(collective_id=0, has_side_effects=True, vmem_limit_bytes=61 * 2**20),
        cost_estimate=pl.CostEstimate(flops=24 * 10**9, bytes_accessed=40 * 10**6, transcendentals=0),
        name="attention_backward",
    )(
        near,
        produced,
        returned_bar.reshape(total, width),
        gate_lines[:, 0, :],
        target_column,
        routes,
        hidden,
        cotangent,
        probs,
        gate,
        gain_two,
        w_router,
        mixed_t,
        w_out,
        tokens,
        gain_one,
        query,
        key_t,
        value,
        weights,
        normed_t,
        w_query,
        w_key,
        w_value,
        buckets,
    )
    steps = 4

    def slab(*form):
        return pl.BlockSpec((form[0] // steps,) + form[1:], lambda g: (g, 0))

    units = up_grad.shape[1]
    matrix = slab(width, width)
    output, up_grad, down_grad, query_grad, key_grad, value_grad, out_grad, router_grad, table_grad, *gains = pl.pallas_call(
        finish_kernel,
        grid=(steps,),
        in_specs=[
            whole((total, width)),
            slab(count, 1),
            slab(count, 1),
            slab(count, width),
            slab(width, units),
            slab(units, width),
            matrix,
            matrix,
            matrix,
            matrix,
            whole(small_shape),
        ],
        out_specs=[
            slab(count, width),
            slab(width, units),
            slab(units, width),
            matrix,
            matrix,
            matrix,
            matrix,
            whole((experts, width)),
            whole((HEADS, BUCKETS)),
            whole((width,)),
            whole((width,)),
        ],
        out_shape=[
            shape((count, width), bf16),
            shape((width, units), f32),
            shape((units, width), f32),
        ]
        + [shape((width, width), f32)] * 4
        + [shape((experts, width), f32), shape((HEADS, BUCKETS), f32)]
        + [shape((width,), f32)] * 2,
        compiler_params=params,
        name="finish",
    )(
        returned.reshape(total, width),
        target_column,
        gate,
        hidden,
        up_grad,
        down_grad,
        query_grad,
        key_grad,
        value_grad,
        out_grad,
        small,
    )
    return (
        output,
        tokens_grad,
        gains[0],
        query_grad,
        key_grad,
        value_grad,
        out_grad,
        table_grad.T,
        gains[1],
        router_grad.T,
        up_grad[None],
        down_grad[None],
    )


def solution(mesh):
    split = P(BOTH, None)
    experts = P(BOTH, None, None)
    in_specs = (split, P(), P(), P(), P(), P(), P(), P(), P(), experts, experts, split, split)
    out_specs = (split, split, P(), P(), P(), P(), P(), P(), P(), P(), experts, experts)
    return jax.shard_map(local, mesh=mesh, in_specs=in_specs, out_specs=out_specs, check_vma=False)
```
